128 devices in a mesh: seq: 32 (over x, y, core), head: 4 (over z).
Axes of the slice: x: 4, y: 4, z: 4, core: 2. Of those that a mesh axis runs over, the one named last changes fastest.
Arguments:
- queries: bfloat16 [49152, 8192], P('seq', 'head'), may hold values from -0.59765625 to 0.59765625
- keys: bfloat16 [49152, 8192], P('seq', 'head'), may hold values from -6 to 6
- values: bfloat16 [49152, 8192], P('seq', 'head'), may hold values from -6 to 6
- doc_start: int32 [49152], P('seq'), may hold values from 0 to 49151, as said below
- norm_gain: float32 [8192], P('head'), may hold values from 0.1 to 1.9
Outputs:
- normed: bfloat16 [49152, 8192], P('seq', 'head')
The draws below stay inside these ranges and needn't reach their ends.
Inputs may be any that keep to these rules, and one draw needn't show every extreme that they name: doc_start[t] <= t and never falls; doc_start[0] = 0; position t begins a document exactly where doc_start[t] = t; 17 documents in all, the first of them at least three quarters of the tokens long, the last a single token.
All inputs are finite; a program needn't handle non-finite values.
Results may differ from the reference program's by a relative error of at most 0.0049.
Values sent between devices are 32-bit elements; how exact they have to be, the bound alone decides.
No kernel may reach another device: no remote copies, remote signals or barrier semaphores. Data moves between devices by JAX's collectives and lax.ppermute only.
A program may use at most 192 MiB of HBM per device.

```python
import jax
import jax.numpy as jnp
from jax import lax

HEADS = 64
DH = 128
GROUP = 256
TOKENS = 49152
DOCS = 17


def draw_doc_start(key, part):
    key = jax.random.fold_in(key, 5)
    first_key = jax.random.fold_in(key, 11)
    rest_key = jax.random.fold_in(key, 12)
    first_cut = jax.random.randint(first_key, (), TOKENS - TOKENS // 4, TOKENS - TOKENS // 8, dtype=jnp.int32)
    offsets = jax.random.permutation(rest_key, TOKENS // 8 - 2)[:DOCS - 3].astype(jnp.int32)
    picked = first_cut + 1 + offsets
    marks = jnp.zeros((TOKENS,), jnp.int32).at[picked].set(1).at[first_cut].set(1).at[0].set(1).at[TOKENS - 1].set(1)
    places = jnp.arange(TOKENS, dtype=jnp.int32)
    return lax.cummax(jnp.where(marks == 1, places, 0), axis=0)


def block_levels(key, shape, cuts, smallest, top_value):
    level = 1.0
    for dim, blocks in cuts:
        draws = jax.random.uniform(jax.random.fold_in(jax.random.fold_in(key, 6), dim), (blocks,), jnp.float32, smallest / len(cuts), top_value / len(cuts))
        level = level * jnp.repeat(jnp.exp(draws), shape[dim] // blocks).reshape((-1,) + (1,) * (len(shape) - 1 - dim))
    return level


def normal_values(own_key, extent, spread, bound, shards=(), kind=jnp.bfloat16):
    gain = block_levels(own_key, extent, shards, -0.22, 0.18) if shards else 1.0
    result = jax.random.normal(own_key, extent, jnp.float32) * spread * gain
    return jnp.minimum(jnp.maximum(result, -bound), bound).astype(kind)


def setup_inputs(seed: int = 0) -> dict:
    arg_keys = jax.random.split(jax.random.key(seed), 6)
    return {
        "queries": normal_values(arg_keys[0], (TOKENS, HEADS * DH), 0.09, 0.59765625, ((0, 32), (1, 4))),
        "keys": normal_values(arg_keys[1], (TOKENS, HEADS * DH), 1.0, 6.0, ((0, 32), (1, 4))),
        "values": normal_values(arg_keys[2], (TOKENS, HEADS * DH), 1.0, 6.0, ((0, 32), (1, 4))),
        "doc_start": draw_doc_start(jax.random.fold_in(arg_keys[5], 71), 0),
        "norm_gain": jnp.clip(1.0 + 0.18 * jax.random.normal(arg_keys[4], (HEADS * DH,), jnp.float32), 0.1, 1.9),
    }


def reference(queries, keys, values, doc_start, norm_gain):
    blocks = TOKENS // GROUP
    qs = queries.reshape(blocks, GROUP, HEADS, DH)
    ks = keys.reshape(blocks, GROUP, HEADS, DH)
    vs = values.reshape(blocks, GROUP, HEADS, DH)
    starts = doc_start.reshape(blocks, GROUP)
    places = jnp.arange(TOKENS, dtype=jnp.int32).reshape(blocks, GROUP)

    def step(carry, inputs):
        qb, kb, vb, sb, pb = inputs
        qf = qb.astype(jnp.float32)
        kf = kb.astype(jnp.float32)
        vf = vb.astype(jnp.float32)
        first = pb[0]
        valid = (pb[None, :] <= pb[:, None]) & (pb[None, :] >= sb[:, None])
        scores = jnp.einsum('thd,jhd->htj', qf, kf)
        scores = jnp.where(valid[None], scores, 0.0).astype(jnp.bfloat16)
        intra = jnp.einsum('htj,jhe->the', scores.astype(jnp.float32), vf)
        carry_b = carry.astype(jnp.bfloat16).astype(jnp.float32)
        inter = jnp.einsum('thd,hde->the', qf, carry_b)
        usable = sb < first
        attn = intra + jnp.where(usable[:, None, None], inter, 0.0)
        attn = attn.reshape(GROUP, HEADS * DH)
        meansq = lax.optimization_barrier(jnp.mean(attn * attn, axis=1, keepdims=True))
        normed = (attn * lax.rsqrt(meansq + 1e-06) * norm_gain[None, :]).astype(jnp.bfloat16)
        last = sb[-1]
        keep = pb >= last
        kept = jnp.where(keep[:, None, None], kf, jnp.zeros_like(kf))
        state = jnp.einsum('jhd,jhe->hde', kept, vf)
        reset = (last >= first).astype(jnp.float32)
        return (state + (1.0 - reset) * carry, normed)
    init = jnp.zeros((HEADS, DH, DH), jnp.float32)
    final, outs = lax.scan(step, init, (qs, ks, vs, starts, places))
    return outs.reshape(TOKENS, HEADS * DH)
```

```python
import functools

import jax
import jax.numpy as jnp
from jax import lax
from jax.experimental import pallas as pl
from jax.experimental.pallas import tpu as pltpu
from jax.sharding import PartitionSpec as P

HEADS = 64
DH = 128
GROUP = 256
EPS = 1e-06
SEQ_Y = 4
SEQ_X = 4
MIB = 1 << 20
CORE, ROW_Y, ROW_X, BASE, FIRST, LAST, CHIP, OPEN = range(8)

ANY = pl.BlockSpec(memory_space=pl.ANY)
VMEM = pl.BlockSpec(memory_space=pltpu.VMEM)
SMEM = pl.BlockSpec(memory_space=pltpu.SMEM)
F32 = jnp.float32


def device_of(x, y, core):
    return (x * SEQ_Y + y) * 2 + core


def places():
    return [(x, y, c) for x in range(SEQ_X) for y in range(SEQ_Y) for c in range(2)]


def swap_cores(value):
    return lax.ppermute(
        value, "seq", [(device_of(x, y, c), device_of(x, y, 1 - c)) for x, y, c in places()]
    )


def turn_row(value, steps):
    return lax.ppermute(
        value,
        "seq",
        [(device_of(x, y, c), device_of(x, (y + steps) % SEQ_Y, c)) for x, y, c in places()],
    )


def next_rows(value, steps):
    return lax.ppermute(
        value,
        "seq",
        [(device_of(x, y, c), device_of(x + steps, y, c)) for x, y, c in places() if x + steps < SEQ_X],
    )


def params(limit, **more):
    return pltpu.CompilerParams(vmem_limit_bytes=limit * MIB, **more)


def state_kernel(meta, k_ref, v_ref, out_ref):
    step = pl.program_id(0)
    tokens, width = k_ref.shape
    rows = meta[BASE] + lax.broadcasted_iota(jnp.int32, (tokens, width), 0)
    kept = jnp.where(rows >= meta[LAST], k_ref[...].astype(F32), 0.0).astype(jnp.bfloat16)
    both = lax.dot_general(kept, v_ref[...], (((0,), (0,)), ((), ())), preferred_element_type=F32)
    at = pl.multiple_of(step * width, width)
    out_ref[pl.ds(at, DH), :] = both[:DH, :DH]
    out_ref[pl.ds(at + DH, DH), :] = both[DH:, DH:]

    @pl.when(step == 0)
    def _():
        row = lax.broadcasted_iota(jnp.int32, (8, DH), 0)
        flags = jnp.where(row == 0, meta[FIRST], meta[LAST])
        out_ref[pl.ds(out_ref.shape[0] - 8, 8), :] = flags.astype(F32)


def half_state(meta, keys, values, other):
    tokens, width = keys.shape
    pairs = width // (4 * DH)

    def at(step, meta):
        half = 1 - meta[CORE] if other else meta[CORE]
        return 0, half * pairs + step

    block = pl.BlockSpec((tokens, 2 * DH), at)
    rows = width // 2 + 8
    return pl.pallas_call(
        state_kernel,
        out_shape=jax.ShapeDtypeStruct((rows, DH), F32),
        grid_spec=pltpu.PrefetchScalarGridSpec(
            num_scalar_prefetch=1,
            grid=(pairs,),
            in_specs=[block, block],
            out_specs=pl.BlockSpec((rows, DH), lambda step, meta: (0, 0)),
        ),
        compiler_params=params(16),
        cost_estimate=pl.CostEstimate(
            flops=2 * tokens * (width // 2) * DH, bytes_accessed=2 * tokens * width, transcendentals=0
        ),
    )(meta, keys, values)


def marks(ref):
    at = ref.shape[0] - 8
    return ref[at : at + 1, :], ref[at + 1 : at + 2, :]


def cores_kernel(meta, keep, recv, own, to1, to2, to3):
    total = keep.shape[0] - 8
    part = total // SEQ_Y
    on_first = meta[CORE] == 0
    k_first, k_last = marks(keep)
    r_first, r_last = marks(recv)
    first = jnp.where(on_first, k_first, r_first)
    last = jnp.where(on_first, r_last, k_last)
    edge = (meta[CHIP] + meta[OPEN]).astype(F32)
    joined = jnp.where(last < edge, 1.0, 0.0)
    w_keep = jnp.where(on_first, joined, 1.0)
    w_recv = jnp.where(on_first, 1.0, joined)
    row = lax.broadcasted_iota(jnp.int32, (8, DH), 0)
    flags = jnp.where(row == 0, first, last)
    for steps, out in enumerate((own, to1, to2, to3)):
        at = pl.multiple_of(lax.rem(meta[ROW_Y] + steps, SEQ_Y) * part, part)
        out[:part, :] = keep[pl.ds(at, part), :] * w_keep + recv[pl.ds(at, part), :] * w_recv
        out[part:, :] = flags


def sources(meta):
    return [lax.rem(meta[ROW_Y] + SEQ_Y - d, SEQ_Y) for d in range(SEQ_Y)]


def ends(meta, place):
    return ((meta[ROW_X] * SEQ_Y + place + 1) * (2 * meta[OPEN])).astype(F32)


def row_kernel(meta, own, from1, from2, from3, out):
    part = out.shape[0]
    refs = (own, from1, from2, from3)
    where = sources(meta)
    row_last = jnp.zeros((1, DH), F32)
    for place, ref in zip(where, refs):
        row_last = row_last + jnp.where(place == SEQ_Y - 1, marks(ref)[1], 0.0)
    total = jnp.zeros((part, DH), F32)
    for place, ref in zip(where, refs):
        total = total + ref[:part, :] * jnp.where(row_last < ends(meta, place), 1.0, 0.0)
    out[...] = total


def carry_kernel(meta, own, from1, from2, from3, up1, up2, up3, out0, out1, out2, out3):
    part = out0.shape[0]
    refs = (own, from1, from2, from3)
    ups = (up1, up2, up3)
    where = sources(meta)
    for steps, out in enumerate((out0, out1, out2, out3)):
        target = (SEQ_Y - steps) % SEQ_Y
        place = where[target]
        first = marks(refs[target])[0]
        total = jnp.zeros((part, DH), F32)
        for source in range(SEQ_Y):
            if source != target:
                before = jnp.where(where[source] < place, 1.0, 0.0)
                weight = jnp.where(first < ends(meta, where[source]), before, 0.0)
                total = total + refs[source][:part, :] * weight
        for back, ref in enumerate(ups):
            edge = ((meta[ROW_X] - back) * (SEQ_Y * 2 * meta[OPEN])).astype(F32)
            total = total + ref[...] * jnp.where(first < edge, 1.0, 0.0)
        out[...] = total


def spread_kernel(meta, own, got1, got2, got3, keep, recv, mine, send):
    part = own.shape[0]
    on_first = meta[CORE] == 0
    second_first = jnp.where(on_first, marks(recv)[0], marks(keep)[0])
    edge = (meta[CHIP] + meta[OPEN]).astype(F32)
    w_state = jnp.where(second_first < edge, 1.0, 0.0)
    w_carry = jnp.where(second_first < meta[CHIP].astype(F32), 1.0, 0.0)
    w_keep = jnp.where(on_first, w_state, 0.0)
    w_recv = jnp.where(on_first, 0.0, w_state)
    for place, ref in zip(sources(meta), (own, got1, got2, got3)):
        at = pl.multiple_of(place * part, part)
        carry = ref[...]
        later = keep[pl.ds(at, part), :] * w_keep + recv[pl.ds(at, part), :] * w_recv + carry * w_carry
        mine[pl.ds(at, part), :] = jnp.where(on_first, carry, later)
        send[pl.ds(at, part), :] = jnp.where(on_first, later, carry)


def small(kernel, meta, args, outs):
    return pl.pallas_call(
        kernel,
        out_shape=[jax.ShapeDtypeStruct((rows, DH), F32) for rows in outs],
        in_specs=[SMEM] + [VMEM] * len(args),
        out_specs=[VMEM] * len(outs),
        compiler_params=params(8),
        cost_estimate=pl.CostEstimate(flops=0, bytes_accessed=2 * MIB, transcendentals=0),
    )(meta, *args)


def local_kernel(meta, starts_ref, q_ref, k_ref, v_ref, out_ref):
    tokens, width = q_ref.shape
    blocks = tokens // GROUP
    carries = [jnp.zeros((DH, DH), F32) for _ in range(width // DH)]
    key_place = lax.broadcasted_iota(jnp.int32, (GROUP, GROUP), 1)
    query_place = lax.broadcasted_iota(jnp.int32, (GROUP, GROUP), 0)
    for block in range(blocks):
        rows = slice(block * GROUP, (block + 1) * GROUP)
        first = meta[BASE] + block * GROUP
        starts = starts_ref[block : block + 1, :]
        column = jnp.broadcast_to(starts, (DH, GROUP)).T
        wide = jnp.concatenate([column, column], axis=1)
        valid = (key_place <= query_place) & (key_place + first >= wide)
        last = starts[:, GROUP - 1 :]
        keep = query_place[:, :DH] + first >= jnp.broadcast_to(last, (GROUP, DH))
        usable = column < first
        go_on = jnp.where(last < first, 1.0, 0.0)
        for head in range(width // DH):
            cols = slice(head * DH, (head + 1) * DH)
            q, k, v = q_ref[rows, cols], k_ref[rows, cols], v_ref[rows, cols]
            scores = lax.dot_general(q, k, (((1,), (1,)), ((), ())), preferred_element_type=F32)
            scores = jnp.where(valid, scores, 0.0).astype(jnp.bfloat16)
            attn = jnp.dot(scores, v, preferred_element_type=F32)
            if block:
                inter = jnp.dot(q, carries[head].astype(jnp.bfloat16), preferred_element_type=F32)
                attn = attn + jnp.where(usable, inter, 0.0)
            out_ref[rows, cols] = attn
            if block < blocks - 1:
                kept = jnp.where(keep, k.astype(F32), 0.0).astype(jnp.bfloat16)
                state = lax.dot_general(kept, v, (((0,), (0,)), ((), ())), preferred_element_type=F32)
                carries[head] = state + go_on * carries[head]


def local_attention(meta, starts, queries, keys, values, chunk, chunks):
    tokens, width = queries.shape
    wide = width // chunks
    steps = wide // (2 * DH)
    block = pl.BlockSpec((tokens, 2 * DH), lambda step, meta: (0, chunk * steps + step))
    heads = wide // DH
    return pl.pallas_call(
        local_kernel,
        out_shape=jax.ShapeDtypeStruct((tokens, wide), F32),
        grid_spec=pltpu.PrefetchScalarGridSpec(
            num_scalar_prefetch=1,
            grid=(steps,),
            in_specs=[pl.BlockSpec(starts.shape, lambda step, meta: (0, 0)), block, block, block],
            out_specs=pl.BlockSpec((tokens, 2 * DH), lambda step, meta: (0, step)),
        ),
        compiler_params=params(24),
        cost_estimate=pl.CostEstimate(
            flops=heads * tokens * (4 * GROUP + 4 * DH) * DH,
            bytes_accessed=tokens * wide * 10,
            transcendentals=0,
        ),
    )(meta, starts, queries, keys, values)


def finish_kernel(meta, *refs, chunks):
    locals_ = refs[:chunks]
    q_ref, mine, got = refs[chunks : chunks + 3]
    outs = refs[chunks + 3 : 2 * chunks + 3]
    squares = refs[2 * chunks + 3]
    states = refs[2 * chunks + 4]
    tokens, width = q_ref.shape
    pairs = width // (2 * DH)
    wide = width // chunks
    on_first = meta[CORE] == 0
    states[...] = jnp.zeros_like(states)
    for pair in range(pairs):
        low = pair < pairs // 2
        at = (pair % (pairs // 2)) * 2 * DH
        for side in range(2):
            rows = slice(at + side * DH, at + (side + 1) * DH)
            one = jnp.where(on_first, mine[rows, :], got[rows, :])
            two = jnp.where(on_first, got[rows, :], mine[rows, :])
            state = one if low else two
            states[pair, side * DH : (side + 1) * DH, side * DH : (side + 1) * DH] = state.astype(jnp.bfloat16)

    def block(index, _):
        at = pl.multiple_of(index * GROUP, GROUP)
        rows = pl.ds(at, GROUP)
        place = at + lax.broadcasted_iota(jnp.int32, (GROUP, 2 * DH), 0)
        usable = place < meta[8]
        total = jnp.zeros((GROUP, DH), F32)
        for pair in range(pairs):
            col = pair * 2 * DH
            cols = slice(col % wide, col % wide + 2 * DH)
            inter = jnp.dot(q_ref[rows, col : col + 2 * DH], states[pair], preferred_element_type=F32)
            attn = locals_[col // wide][rows, cols] + jnp.where(usable, inter, 0.0)
            outs[col // wide][rows, cols] = attn
            total = total + attn[:, :DH] * attn[:, :DH] + attn[:, DH:] * attn[:, DH:]
        squares[:, pl.ds(at, GROUP)] = jnp.sum(total.T, axis=0, keepdims=True)
        return 0

    lax.fori_loop(0, tokens // GROUP, block, 0)


def finish(meta, locals_, queries, mine, got):
    tokens, width = queries.shape
    chunks = len(locals_)
    wide = width // chunks
    *outs, squares = pl.pallas_call(
        functools.partial(finish_kernel, chunks=chunks),
        out_shape=[pltpu.VMEM((tokens, wide), F32)] * chunks + [jax.ShapeDtypeStruct((1, tokens), F32)],
        in_specs=[SMEM] + [VMEM] * (chunks + 3),
        out_specs=[VMEM] * (chunks + 1),
        scratch_shapes=[pltpu.VMEM((width // (2 * DH), 2 * DH, 2 * DH), jnp.bfloat16)],
        input_output_aliases={1 + c: c for c in range(chunks)},
        compiler_params=params(24),
        cost_estimate=pl.CostEstimate(
            flops=2 * tokens * width * DH, bytes_accessed=tokens * width * 6, transcendentals=0
        ),
    )(meta, *[pltpu.with_memory_space_constraint(v, pltpu.VMEM) for v in locals_], pltpu.with_memory_space_constraint(queries, pltpu.VMEM), mine, got)
    return outs, squares


def norm_kernel(total_ref, gain_ref, *refs, chunks, rows):
    ins = refs[:chunks]
    out, buffer, sems = refs[chunks:]
    tokens = ins[0].shape[0]
    wide = ins[0].shape[1]
    width = wide * chunks

    def copy(index, slot):
        return pltpu.make_async_copy(
            buffer.at[slot], out.at[pl.ds(index * rows, rows), :], sems.at[slot]
        )

    steps = tokens // rows
    for index in range(steps):
        slot = index % 2
        if index >= 2:
            copy(index - 2, slot).wait()
        span = slice(index * rows, (index + 1) * rows)
        mean = total_ref[:, span] / float(HEADS * DH)
        factor = jnp.broadcast_to(lax.rsqrt(mean + EPS), (DH, rows)).T
        for col in range(0, width, DH):
            cols = slice(col % wide, col % wide + DH)
            value = ins[col // wide][span, cols] * factor * gain_ref[:, col : col + DH]
            buffer[slot, :, col : col + DH] = value.astype(jnp.bfloat16)
        copy(index, slot).start()
    for index in range(steps - 2, steps):
        copy(index, index % 2).wait()


def normalise(total, gain, parts):
    tokens, wide = parts[0].shape
    chunks = len(parts)
    width = wide * chunks
    rows = 128
    return pl.pallas_call(
        functools.partial(norm_kernel, chunks=chunks, rows=rows),
        out_shape=jax.ShapeDtypeStruct((tokens, width), jnp.bfloat16),
        in_specs=[VMEM] * (chunks + 2),
        out_specs=ANY,
        scratch_shapes=[pltpu.VMEM((2, rows, width), jnp.bfloat16), pltpu.SemaphoreType.DMA((2,))],
        compiler_params=params(16),
        cost_estimate=pl.CostEstimate(flops=2 * tokens * width, bytes_accessed=6 * tokens * width, transcendentals=0),
    )(total, gain, *[pltpu.with_memory_space_constraint(v, pltpu.VMEM) for v in parts])


def on_device(queries, keys, values, doc_start, norm_gain):
    tokens, width = queries.shape
    seq = lax.axis_index("seq")
    base = seq * tokens
    core = lax.rem(seq, 2)
    chip = seq // 2
    meta = jnp.stack(
        [core, lax.rem(chip, SEQ_Y), chip // SEQ_Y, base, doc_start[0], doc_start[-1], chip * 2 * tokens, jnp.int32(tokens)]
    )
    opened = jnp.sum((doc_start < base).astype(jnp.int32))
    full_meta = jnp.concatenate([meta, opened[None]])
    starts = doc_start.reshape(tokens // GROUP, GROUP)

    away = half_state(meta, keys, values, True)
    recv = swap_cores(away)
    keep = half_state(meta, keys, values, False)
    part = (keep.shape[0] - 8) // SEQ_Y

    chunks = 4
    local = functools.partial(local_attention, meta, starts, queries, keys, values, chunks=chunks)

    mine = small(cores_kernel, meta, (keep, recv), [part + 8] * SEQ_Y)
    rows = [mine[0]] + [turn_row(mine[d], d) for d in (1, 2, 3)]
    locals_ = [local(0), local(1)]
    (whole,) = small(row_kernel, meta, rows, [part])
    ups = [next_rows(whole, d) for d in (1, 2, 3)]
    locals_.append(local(2))
    carries = small(carry_kernel, meta, (*rows, *ups), [part] * SEQ_Y)
    got = [carries[0]] + [turn_row(carries[d], d) for d in (1, 2, 3)]
    locals_.append(local(3))
    own, send = small(spread_kernel, meta, (*got, keep, recv), [part * SEQ_Y] * 2)
    other = swap_cores(send)
    parts, squares = finish(full_meta, locals_, queries, own, other)
    total = lax.psum(squares, "head")
    return normalise(total, norm_gain.reshape(1, width), parts)


def solution(mesh):
    return jax.shard_map(
        on_device,
        mesh=mesh,
        in_specs=(P("seq", "head"), P("seq", "head"), P("seq", "head"), P("seq"), P("head")),
        out_specs=P("seq", "head"),
        check_vma=False,
    )
```

```python
import functools

import jax
import jax.numpy as jnp
from jax import lax
from jax.experimental import pallas as pl
from jax.experimental.pallas import tpu as pltpu
from jax.sharding import PartitionSpec as P

HEADS = 64
DH = 128
GROUP = 256
EPS = 1e-06
SEQ_Y = 4
SEQ_X = 4
MIB = 1 << 20
ANY = pl.BlockSpec(memory_space=pl.ANY)
VMEM = pl.BlockSpec(memory_space=pltpu.VMEM)
SMEM = pl.BlockSpec(memory_space=pltpu.SMEM)
F32 = jnp.float32


def device_of(x, y, core):
    return (x * SEQ_Y + y) * 2 + core


def places():
    return [(x, y, c) for x in range(SEQ_X) for y in range(SEQ_Y) for c in range(2)]


def swap_cores(value):
    return lax.ppermute(
        value, "seq", [(device_of(x, y, c), device_of(x, y, 1 - c)) for x, y, c in places()]
    )


def turn_row(value, steps):
    return lax.ppermute(
        value,
        "seq",
        [(device_of(x, y, c), device_of(x, (y + steps) % SEQ_Y, c)) for x, y, c in places()],
    )


def swap_rows(value, steps):
    return lax.ppermute(
        value, "seq", [(device_of(x, y, c), device_of(x ^ steps, y, c)) for x, y, c in places()]
    )


def params(limit):
    return pltpu.CompilerParams(vmem_limit_bytes=limit * MIB)


def in_hbm(value):
    return pltpu.with_memory_space_constraint(value, pltpu.HBM)


def in_vmem(value):
    return pltpu.with_memory_space_constraint(value, pltpu.VMEM)


def after(value, *others):
    return lax.optimization_barrier((value, *others))[0]


def spot():
    seq = lax.axis_index("seq")
    chip = lax.div(seq, 2)
    return lax.rem(seq, 2), lax.rem(chip, SEQ_Y), lax.div(chip, SEQ_Y), seq


def halves(core, half):
    return [pl.multiple_of(side * half, half) for side in (1 - core, core)]


def state_kernel(starts_hbm, k_hbm, v_hbm, away, keep, k_ref, v_ref, starts, sems, starts_sem):
    tokens, width = k_ref.shape
    half = width // 2
    core, _, _, seq = spot()
    base = seq * tokens
    steps = tokens // GROUP
    starts_copy = pltpu.make_async_copy(starts_hbm, starts.at[0], starts_sem)

    def copies(step):
        rows = pl.ds(pl.multiple_of(step * GROUP, GROUP), GROUP)
        return [
            pltpu.make_async_copy(source.at[rows, :], ref.at[rows, :], sems.at[index, step])
            for index, (source, ref) in enumerate(((k_hbm, k_ref), (v_hbm, v_ref)))
        ]

    starts_copy.start()
    for step in range(steps):
        for copy in copies(step):
            copy.start()
    for out in (away, keep):
        out[...] = jnp.zeros_like(out)
    row = lax.broadcasted_iota(jnp.int32, (8, DH), 0)
    place = lax.broadcasted_iota(jnp.int32, (GROUP, 2 * DH), 0)
    starts_copy.wait()
    first = jnp.broadcast_to(starts[:, :1], (1, DH))
    last = jnp.broadcast_to(starts[:, tokens - 1 :], (1, DH))
    for out in (away, keep):
        out[half:, :] = jnp.where(row == 0, first, last).astype(F32)
    last = jnp.broadcast_to(jnp.concatenate([last, last], axis=1), (GROUP, 2 * DH))

    def body(step, _):
        for copy in copies(step):
            copy.wait()
        at = pl.multiple_of(step * GROUP, GROUP)
        rows = pl.ds(at, GROUP)
        kept = jnp.where(base + at + place >= last, 1.0, 0.0).astype(jnp.bfloat16)
        for out, side in zip((away, keep), halves(core, half)):
            for col in range(0, half, 2 * DH):
                cols = pl.ds(side + col, 2 * DH)
                both = lax.dot_general(
                    k_ref[rows, cols] * kept, v_ref[rows, cols], (((0,), (0,)), ((), ())), preferred_element_type=F32
                )
                out[col : col + DH, :] += both[:DH, :DH]
                out[col + DH : col + 2 * DH, :] += both[DH:, DH:]
        return 0

    lax.fori_loop(0, steps, body, 0)


def own_states(starts, keys, values):
    tokens, width = keys.shape
    state = pltpu.VMEM((width // 2 + 8, DH), F32)
    held = pltpu.VMEM((tokens, width), jnp.bfloat16)
    return pl.pallas_call(
        state_kernel,
        out_shape=[state, state, held, held, pltpu.VMEM((1, tokens), jnp.int32)],
        in_specs=[ANY, ANY, ANY],
        out_specs=[VMEM] * 5,
        scratch_shapes=[
            pltpu.SemaphoreType.DMA((2, tokens // GROUP)),
            pltpu.SemaphoreType.DMA,
        ],
        compiler_params=params(4),
        cost_estimate=pl.CostEstimate(
            flops=2 * tokens * width * DH, bytes_accessed=4 * tokens * width, transcendentals=0
        ),
    )(in_hbm(starts), in_hbm(keys), in_hbm(values))


def marks(ref):
    at = ref.shape[0] - 8
    return ref[at : at + 1, :], ref[at + 1 : at + 2, :]


def chip_edges(tokens, seq):
    first = lax.div(seq, 2) * (2 * tokens)
    return first.astype(F32), (first + tokens).astype(F32)


def cores_kernel(keep, recv, own, to1, to2, to3, *, tokens):
    total = keep.shape[0] - 8
    part = total // SEQ_Y
    core, y, _, seq = spot()
    on_first = core == 0
    k_first, k_last = marks(keep)
    r_first, r_last = marks(recv)
    first = jnp.where(on_first, k_first, r_first)
    last = jnp.where(on_first, r_last, k_last)
    edge = chip_edges(tokens, seq)[1]
    joined = jnp.where(last < edge, 1.0, 0.0)
    w_keep = jnp.where(on_first, joined, 1.0)
    w_recv = jnp.where(on_first, 1.0, joined)
    row = lax.broadcasted_iota(jnp.int32, (8, DH), 0)
    flags = jnp.where(row == 0, first, last)
    for steps, out in enumerate((own, to1, to2, to3)):
        at = pl.multiple_of(lax.rem(y + steps, SEQ_Y) * part, part)
        out[:part, :] = keep[pl.ds(at, part), :] * w_keep + recv[pl.ds(at, part), :] * w_recv
        out[part:, :] = flags


def sources(y):
    return [lax.rem(y + SEQ_Y - d, SEQ_Y) for d in range(SEQ_Y)]


def ends(tokens, x, place):
    return ((x * SEQ_Y + place + 1) * (2 * tokens)).astype(F32)


def row_kernel(own, from1, from2, from3, out, *, tokens):
    part = out.shape[0]
    refs = (own, from1, from2, from3)
    _, y, x, _ = spot()
    where = sources(y)
    row_last = jnp.zeros((1, DH), F32)
    for place, ref in zip(where, refs):
        row_last = row_last + jnp.where(place == SEQ_Y - 1, marks(ref)[1], 0.0)
    total = jnp.zeros((part, DH), F32)
    for place, ref in zip(where, refs):
        total = total + ref[:part, :] * jnp.where(row_last < ends(tokens, x, place), 1.0, 0.0)
    out[...] = total


def carry_kernel(own, from1, from2, from3, up3, up2, up1, out0, out1, out2, out3, *, tokens):
    part = out0.shape[0]
    refs = (own, from1, from2, from3)
    ups = (up3, up2, up1)
    _, y, x, _ = spot()
    where = sources(y)
    for steps, out in enumerate((out0, out1, out2, out3)):
        target = (SEQ_Y - steps) % SEQ_Y
        place = where[target]
        first = marks(refs[target])[0]
        total = jnp.zeros((part, DH), F32)
        for source in range(SEQ_Y):
            if source != target:
                before = jnp.where(where[source] < place, 1.0, 0.0)
                weight = jnp.where(first < ends(tokens, x, where[source]), before, 0.0)
                total = total + refs[source][:part, :] * weight
        for steps, ref in zip((3, 2, 1), ups):
            row = x ^ steps
            before = jnp.where(row < x, 1.0, 0.0)
            total = total + ref[...] * jnp.where(first < ends(tokens, row, SEQ_Y - 1), before, 0.0)
        out[...] = total


def spread_kernel(own, got1, got2, got3, keep, recv, mine, send, *, tokens):
    part = own.shape[0]
    core, y, _, seq = spot()
    on_first = core == 0
    chip, edge = chip_edges(tokens, seq)
    second_first = jnp.where(on_first, marks(recv)[0], marks(keep)[0])
    w_state = jnp.where(second_first < edge, 1.0, 0.0)
    w_carry = jnp.where(second_first < chip, 1.0, 0.0)
    w_keep = jnp.where(on_first, w_state, 0.0)
    w_recv = jnp.where(on_first, 0.0, w_state)
    for place, ref in zip(sources(y), (own, got1, got2, got3)):
        at = pl.multiple_of(place * part, part)
        carry = ref[...]
        later = keep[pl.ds(at, part), :] * w_keep + recv[pl.ds(at, part), :] * w_recv + carry * w_carry
        mine[pl.ds(at, part), :] = jnp.where(on_first, carry, later)
        send[pl.ds(at, part), :] = jnp.where(on_first, later, carry)


def small(kernel, tokens, args, outs):
    return pl.pallas_call(
        functools.partial(kernel, tokens=tokens),
        out_shape=[jax.ShapeDtypeStruct((rows, DH), F32) for rows in outs],
        in_specs=[VMEM] * len(args),
        out_specs=[VMEM] * len(outs),
        compiler_params=params(4),
        cost_estimate=pl.CostEstimate(flops=0, bytes_accessed=2 * MIB, transcendentals=0),
    )(*args)


def local_kernel(starts_ref, q_ref, k_ref, v_ref, out_ref, *, kept, column):
    tokens, width = out_ref.shape
    core, _, _, seq = spot()
    side = halves(core, q_ref.shape[1] // 2)[kept] + column
    key_place = lax.broadcasted_iota(jnp.int32, (GROUP, GROUP), 1)
    query_place = lax.broadcasted_iota(jnp.int32, (GROUP, GROUP), 0)
    blocks = tokens // GROUP
    carries = [None] * (width // DH)
    for block in range(blocks):
        rows = slice(block * GROUP, (block + 1) * GROUP)
        first = seq * tokens + block * GROUP
        starts = starts_ref[:, rows]
        begin = jnp.broadcast_to(starts, (DH, GROUP)).T
        valid = (key_place <= query_place) & (key_place + first >= jnp.concatenate([begin, begin], axis=1))
        last = starts[:, GROUP - 1 :]
        keep = query_place[:, :DH] + first >= jnp.broadcast_to(last, (GROUP, DH))
        keep = jnp.where(keep, 1.0, 0.0).astype(jnp.bfloat16)
        usable = jnp.where(begin < first, 1.0, 0.0).astype(jnp.bfloat16)
        go_on = jnp.where(last < first, 1.0, 0.0)
        for head in range(width // DH):
            cols = pl.ds(side + head * DH, DH)
            q, k, v = q_ref[rows, cols], k_ref[rows, cols], v_ref[rows, cols]
            scores = lax.dot_general(q, k, (((1,), (1,)), ((), ())), preferred_element_type=F32)
            scores = jnp.where(valid, scores, 0.0).astype(jnp.bfloat16)
            if block < blocks - 1:
                both = jnp.dot(
                    jnp.concatenate([scores, (k * keep).T], axis=0), v, preferred_element_type=F32
                )
                attn, state = both[:GROUP], both[GROUP:]
            else:
                attn, state = jnp.dot(scores, v, preferred_element_type=F32), None
            if block:
                attn = attn + jnp.dot(q * usable, carries[head].astype(jnp.bfloat16), preferred_element_type=F32)
            out_ref[rows, head * DH : (head + 1) * DH] = attn
            if state is not None:
                carries[head] = state if block == 0 else state + go_on * carries[head]


def local_attention(starts, queries, keys, values, kept, column, wide):
    tokens = queries.shape[0]
    return pl.pallas_call(
        functools.partial(local_kernel, kept=kept, column=column),
        out_shape=pltpu.VMEM((tokens, wide), F32),
        in_specs=[VMEM] * 4,
        out_specs=VMEM,
        compiler_params=params(4),
        cost_estimate=pl.CostEstimate(
            flops=wide * tokens * (4 * GROUP + 4 * DH), bytes_accessed=tokens * wide * 10, transcendentals=0
        ),
    )(starts, in_vmem(queries), in_vmem(keys), in_vmem(values))


def finish_kernel(starts_ref, q_ref, *refs, sizes, rows):
    count = len(sizes)
    locals_, (away, own) = refs[:count], refs[count : count + 2]
    outs, squares, states = refs[count + 2 : 2 * count + 2], refs[2 * count + 2], refs[2 * count + 3]
    tokens, width = q_ref.shape
    half = width // 2
    core, _, _, seq = spot()
    opened = jnp.sum((starts_ref[...] < seq * tokens).astype(jnp.int32))
    pairs = []
    for index, size in enumerate(sizes):
        for col in range(0, size, 2 * DH):
            pairs.append((index, col))
    states[...] = jnp.zeros_like(states)
    for pair in range(len(pairs)):
        source = away if pair < len(pairs) // 2 else own
        at = pair * 2 * DH % half
        for side in range(2):
            span = slice(side * DH, (side + 1) * DH)
            states[pair, span, span] = source[at + side * DH : at + (side + 1) * DH, :].astype(jnp.bfloat16)
    sides = halves(core, half)

    def step(index, _):
        start = pl.multiple_of(index * rows, rows)
        span = pl.ds(start, rows)
        usable = start + lax.broadcasted_iota(jnp.int32, (rows, 2 * DH), 0) < opened
        total = jnp.zeros((rows, DH), F32)
        for pair, (part, col) in enumerate(pairs):
            side = sides[pair // (len(pairs) // 2)]
            q = q_ref[span, pl.ds(side + pair * 2 * DH % half, 2 * DH)]
            inter = jnp.dot(q, states[pair], preferred_element_type=F32)
            cols = slice(col, col + 2 * DH)
            attn = locals_[part][span, cols] + jnp.where(usable, inter, 0.0)
            outs[part][span, cols] = attn
            total = total + attn[:, :DH] * attn[:, :DH] + attn[:, DH:] * attn[:, DH:]
        squares[:, span] = jnp.sum(total.T, axis=0, keepdims=True)
        return 0

    lax.fori_loop(0, tokens // rows, step, 0)


def finish(starts, queries, locals_, away, own):
    tokens, width = queries.shape
    sizes = [part.shape[1] for part in locals_]
    count = len(sizes)
    *outs, squares = pl.pallas_call(
        functools.partial(finish_kernel, sizes=sizes, rows=2 * GROUP),
        out_shape=[pltpu.VMEM((tokens, size), F32) for size in sizes] + [jax.ShapeDtypeStruct((1, tokens), F32)],
        in_specs=[VMEM] * (count + 4),
        out_specs=[VMEM] * (count + 1),
        scratch_shapes=[pltpu.VMEM((width // (2 * DH), 2 * DH, 2 * DH), jnp.bfloat16)],
        compiler_params=params(8),
        cost_estimate=pl.CostEstimate(
            flops=2 * tokens * width * DH, bytes_accessed=tokens * width * 6, transcendentals=0
        ),
    )(starts, in_vmem(queries), *[in_vmem(part) for part in locals_], away, own)
    return outs, squares


def norm_kernel(sq0, sq1, sq2, sq3, gain_ref, *refs, sizes, rows):
    count = len(sizes)
    ins = refs[:count]
    out, buffer, sems = refs[count:]
    tokens, width = out.shape
    half = width // 2
    core = spot()[0]
    sides = halves(core, half)
    places = []
    for index, size in enumerate(sizes):
        for col in range(0, size, DH):
            places.append((index, col))

    def copy(index):
        at = pl.ds(pl.multiple_of(index * rows, rows), rows)
        return pltpu.make_async_copy(buffer.at[at, :], out.at[at, :], sems.at[index])

    def step(index, _):
        span = pl.ds(pl.multiple_of(index * rows, rows), rows)
        total = (sq0[:, span] + sq1[:, span]) + (sq2[:, span] + sq3[:, span])
        factor = jnp.broadcast_to(lax.rsqrt(total / (HEADS * DH) + EPS), (DH, rows)).T
        for number, (index_in, col) in enumerate(places):
            side = sides[number // (len(places) // 2)]
            cols = pl.ds(side + number * DH % half, DH)
            value = ins[index_in][span, col : col + DH] * factor * gain_ref[:, cols]
            buffer[span, cols] = value.astype(jnp.bfloat16)
        copy(index).start()
        return 0

    steps = tokens // rows
    lax.fori_loop(0, steps, step, 0)
    for index in range(steps):
        copy(index).wait()


def normalise(squares, gain, parts):
    tokens = parts[0].shape[0]
    sizes = [part.shape[1] for part in parts]
    width = sum(sizes)
    rows = 2 * DH
    return pl.pallas_call(
        functools.partial(norm_kernel, sizes=sizes, rows=rows),
        out_shape=jax.ShapeDtypeStruct((tokens, width), jnp.bfloat16),
        in_specs=[VMEM] * (len(sizes) + 5),
        out_specs=ANY,
        scratch_shapes=[
            pltpu.VMEM((tokens, width), jnp.bfloat16),
            pltpu.SemaphoreType.DMA((tokens // rows,)),
        ],
        compiler_params=params(8),
        cost_estimate=pl.CostEstimate(flops=2 * tokens * width, bytes_accessed=6 * tokens * width, transcendentals=0),
    )(*squares, gain, *[in_vmem(part) for part in parts])


def on_device(queries, keys, values, doc_start, norm_gain):
    tokens, width = queries.shape
    half = width // 2

    away, keep, keys, values, starts = own_states(doc_start, keys, values)
    recv = swap_cores(away)
    queries = after(queries, away)
    part = half // SEQ_Y

    def local(kept, column, wide, gate):
        return local_attention(after(starts, gate), queries, keys, values, kept, column, wide)

    mine = small(cores_kernel, tokens, (keep, recv), [part + 8] * SEQ_Y)
    rows = [mine[0]] + [turn_row(mine[d], d) for d in (1, 2, 3)]
    first = local(0, 0, 3 * half // 4, mine[0])
    rows[3], first = lax.optimization_barrier((rows[3], first))
    (whole,) = small(row_kernel, tokens, rows, [part])
    ups = [swap_rows(whole, d) for d in (3, 2, 1)]
    third = local(1, 0, half // 2, whole)
    ups[2], third = lax.optimization_barrier((ups[2], third))
    carries = small(carry_kernel, tokens, (*rows, *ups), [part] * SEQ_Y)
    got = [carries[0]] + [turn_row(carries[d], d) for d in (1, 2, 3)]
    fourth = local(1, half // 2, half // 2, carries[0])
    got[3], fourth = lax.optimization_barrier((got[3], fourth))
    own, send = small(spread_kernel, tokens, (*got, keep, recv), [part * SEQ_Y] * 2)
    other = swap_cores(send)
    second = local(0, 3 * half // 4, half // 4, own)
    parts, squares = finish(starts, queries, [first, second, third, fourth], other, own)
    sums = [squares] + [
        lax.ppermute(squares, "head", [(z, z ^ d) for z in range(4)]) for d in (3, 2, 1)
    ]
    return normalise(sums, norm_gain.reshape(1, width), parts)


def solution(mesh):
    return jax.shard_map(
        on_device,
        mesh=mesh,
        in_specs=(P("seq", "head"), P("seq", "head"), P("seq", "head"), P("seq"), P("head")),
        out_specs=P("seq", "head"),
        check_vma=False,
    )
```

```python
import functools

import jax
import jax.numpy as jnp
from jax import lax
from jax.experimental import pallas as pl
from jax.experimental.pallas import tpu as pltpu
from jax.sharding import PartitionSpec as P

HEADS = 64
DH = 128
GROUP = 256
EPS = 1e-06
SEQ_Y = 4
SEQ_X = 4
MIB = 1 << 20
ANY = pl.BlockSpec(memory_space=pl.ANY)
VMEM = pl.BlockSpec(memory_space=pltpu.VMEM)
SMEM = pl.BlockSpec(memory_space=pltpu.SMEM)
F32 = jnp.float32


def device_of(x, y, core):
    return (x * SEQ_Y + y) * 2 + core


def places():
    return [(x, y, c) for x in range(SEQ_X) for y in range(SEQ_Y) for c in range(2)]


def swap_cores(value):
    return lax.ppermute(
        value, "seq", [(device_of(x, y, c), device_of(x, y, 1 - c)) for x, y, c in places()]
    )


def turn_row(value, steps):
    return lax.ppermute(
        value,
        "seq",
        [(device_of(x, y, c), device_of(x, (y + steps) % SEQ_Y, c)) for x, y, c in places()],
    )


def swap_rows(value, steps):
    return lax.ppermute(
        value, "seq", [(device_of(x, y, c), device_of(x ^ steps, y, c)) for x, y, c in places()]
    )


def params(limit):
    return pltpu.CompilerParams(vmem_limit_bytes=limit * MIB)


def in_hbm(value):
    return pltpu.with_memory_space_constraint(value, pltpu.HBM)


def in_vmem(value):
    return pltpu.with_memory_space_constraint(value, pltpu.VMEM)


def after(value, *others):
    return lax.optimization_barrier((value, *others))[0]


def spot():
    seq = lax.axis_index("seq")
    chip = lax.div(seq, 2)
    return lax.rem(seq, 2), lax.rem(chip, SEQ_Y), lax.div(chip, SEQ_Y), seq


def halves(core, half):
    return [pl.multiple_of(side * half, half) for side in (1 - core, core)]


def state_kernel(starts_hbm, k_hbm, v_hbm, away, k_ref, v_ref, starts, sems, starts_sem, *, rows):
    tokens, width = k_ref.shape
    half = width // 2
    core, _, _, seq = spot()
    base = seq * tokens
    starts_copy = pltpu.make_async_copy(starts_hbm, starts.at[0], starts_sem)
    spans = [slice(start, start + rows) for start in range(0, tokens, rows)]
    copies = [
        [
            pltpu.make_async_copy(
                source.at[span, pl.ds(side, half)],
                ref.at[span, index * half : (index + 1) * half],
                sems.at[2 * number + index, step],
            )
            for number, (source, ref) in enumerate(((k_hbm, k_ref), (v_hbm, v_ref)))
        ]
        for index, side in enumerate(halves(core, half))
        for step, span in enumerate(spans)
    ]
    starts_copy.start()
    for group in copies:
        for copy in group:
            copy.start()
    row = lax.broadcasted_iota(jnp.int32, (8, DH), 0)
    place = base + lax.broadcasted_iota(jnp.int32, (rows, 2 * DH), 0)
    starts_copy.wait()
    first = jnp.broadcast_to(starts[:, :1], (1, DH))
    last = jnp.broadcast_to(starts[:, tokens - 1 :], (1, DH))
    away[half:, :] = jnp.where(row == 0, first, last).astype(F32)
    last = jnp.broadcast_to(starts[:, tokens - 1 :], (rows, 2 * DH))
    for step, span in enumerate(spans):
        for copy in copies[step]:
            copy.wait()
        kept = jnp.where(place + step * rows >= last, 1.0, 0.0).astype(jnp.bfloat16)
        add_states(away, k_ref, v_ref, span, kept, 0, step == 0)
    for group in copies[len(spans) :]:
        for copy in group:
            copy.wait()


def add_states(out, k_ref, v_ref, span, kept, column, first):
    for col in range(0, out.shape[0] - 8, 2 * DH):
        cols = slice(column + col, column + col + 2 * DH)
        both = lax.dot_general(
            k_ref[span, cols] * kept, v_ref[span, cols], (((0,), (0,)), ((), ())), preferred_element_type=F32
        )
        for head in range(2):
            lanes = slice(head * DH, (head + 1) * DH)
            at = slice(col + head * DH, col + (head + 1) * DH)
            if first:
                out[at, :] = both[lanes, lanes]
            else:
                out[at, :] += both[lanes, lanes]


def keep_kernel(starts, k_ref, v_ref, keep, *, rows):
    tokens, width = k_ref.shape
    half = width // 2
    base = spot()[3] * tokens
    row = lax.broadcasted_iota(jnp.int32, (8, DH), 0)
    first = jnp.broadcast_to(starts[:, :1], (1, DH))
    last = jnp.broadcast_to(starts[:, tokens - 1 :], (1, DH))
    keep[half:, :] = jnp.where(row == 0, first, last).astype(F32)
    place = base + lax.broadcasted_iota(jnp.int32, (rows, 2 * DH), 0)
    last = jnp.broadcast_to(starts[:, tokens - 1 :], (rows, 2 * DH))
    for start in range(0, tokens, rows):
        kept = jnp.where(place + start >= last, 1.0, 0.0).astype(jnp.bfloat16)
        add_states(keep, k_ref, v_ref, slice(start, start + rows), kept, half, start == 0)


def own_states(starts, keys, values):
    tokens, width = keys.shape
    rows = 6 * GROUP
    held = pltpu.VMEM((tokens, width), jnp.bfloat16)
    return pl.pallas_call(
        functools.partial(state_kernel, rows=rows),
        out_shape=[pltpu.VMEM((width // 2 + 8, DH), F32), held, held, pltpu.VMEM((1, tokens), jnp.int32)],
        in_specs=[ANY, ANY, ANY],
        out_specs=[VMEM] * 4,
        scratch_shapes=[pltpu.SemaphoreType.DMA((4, tokens // rows)), pltpu.SemaphoreType.DMA],
        compiler_params=params(4),
        cost_estimate=pl.CostEstimate(
            flops=tokens * width * DH, bytes_accessed=4 * tokens * width, transcendentals=0
        ),
    )(in_hbm(starts), in_hbm(keys), in_hbm(values))


def kept_states(starts, keys, values):
    tokens, width = keys.shape
    return pl.pallas_call(
        functools.partial(keep_kernel, rows=2 * GROUP),
        out_shape=pltpu.VMEM((width // 2 + 8, DH), F32),
        in_specs=[VMEM] * 3,
        out_specs=VMEM,
        compiler_params=params(4),
        cost_estimate=pl.CostEstimate(flops=tokens * width * DH, bytes_accessed=2 * tokens * width, transcendentals=0),
    )(starts, in_vmem(keys), in_vmem(values))


def marks(ref):
    at = ref.shape[0] - 8
    return ref[at : at + 1, :], ref[at + 1 : at + 2, :]


def chip_edges(tokens, seq):
    first = lax.div(seq, 2) * (2 * tokens)
    return first.astype(F32), (first + tokens).astype(F32)


def cores_kernel(keep, recv, own, to1, to2, to3, *, tokens):
    total = keep.shape[0] - 8
    part = total // SEQ_Y
    core, y, _, seq = spot()
    on_first = core == 0
    k_first, k_last = marks(keep)
    r_first, r_last = marks(recv)
    first = jnp.where(on_first, k_first, r_first)
    last = jnp.where(on_first, r_last, k_last)
    edge = chip_edges(tokens, seq)[1]
    joined = jnp.where(last < edge, 1.0, 0.0)
    w_keep = jnp.where(on_first, joined, 1.0)
    w_recv = jnp.where(on_first, 1.0, joined)
    row = lax.broadcasted_iota(jnp.int32, (8, DH), 0)
    flags = jnp.where(row == 0, first, last)
    for steps, out in enumerate((own, to1, to2, to3)):
        at = pl.multiple_of(lax.rem(y + steps, SEQ_Y) * part, part)
        out[:part, :] = keep[pl.ds(at, part), :] * w_keep + recv[pl.ds(at, part), :] * w_recv
        out[part:, :] = flags


def sources(y):
    return [lax.rem(y + SEQ_Y - d, SEQ_Y) for d in range(SEQ_Y)]


def ends(tokens, x, place):
    return ((x * SEQ_Y + place + 1) * (2 * tokens)).astype(F32)


def row_kernel(own, from1, from2, from3, out, *, tokens):
    part = out.shape[0]
    refs = (own, from1, from2, from3)
    _, y, x, _ = spot()
    where = sources(y)
    row_last = jnp.zeros((1, DH), F32)
    for place, ref in zip(where, refs):
        row_last = row_last + jnp.where(place == SEQ_Y - 1, marks(ref)[1], 0.0)
    total = jnp.zeros((part, DH), F32)
    for place, ref in zip(where, refs):
        total = total + ref[:part, :] * jnp.where(row_last < ends(tokens, x, place), 1.0, 0.0)
    out[...] = total


def carry_kernel(own, from1, from2, from3, up3, up2, up1, out0, out1, out2, out3, *, tokens):
    part = out0.shape[0]
    refs = (own, from1, from2, from3)
    ups = (up3, up2, up1)
    _, y, x, _ = spot()
    where = sources(y)
    for steps, out in enumerate((out0, out1, out2, out3)):
        target = (SEQ_Y - steps) % SEQ_Y
        place = where[target]
        first = marks(refs[target])[0]
        total = jnp.zeros((part, DH), F32)
        for source in range(SEQ_Y):
            if source != target:
                before = jnp.where(where[source] < place, 1.0, 0.0)
                weight = jnp.where(first < ends(tokens, x, where[source]), before, 0.0)
                total = total + refs[source][:part, :] * weight
        for steps, ref in zip((3, 2, 1), ups):
            row = x ^ steps
            before = jnp.where(row < x, 1.0, 0.0)
            total = total + ref[...] * jnp.where(first < ends(tokens, row, SEQ_Y - 1), before, 0.0)
        out[...] = total


def spread_kernel(own, got1, got2, got3, keep, recv, mine, send, *, tokens):
    part = own.shape[0]
    core, y, _, seq = spot()
    on_first = core == 0
    chip, edge = chip_edges(tokens, seq)
    second_first = jnp.where(on_first, marks(recv)[0], marks(keep)[0])
    w_state = jnp.where(second_first < edge, 1.0, 0.0)
    w_carry = jnp.where(second_first < chip, 1.0, 0.0)
    w_keep = jnp.where(on_first, w_state, 0.0)
    w_recv = jnp.where(on_first, 0.0, w_state)
    for place, ref in zip(sources(y), (own, got1, got2, got3)):
        at = pl.multiple_of(place * part, part)
        carry = ref[...]
        later = keep[pl.ds(at, part), :] * w_keep + recv[pl.ds(at, part), :] * w_recv + carry * w_carry
        mine[pl.ds(at, part), :] = jnp.where(on_first, carry, later)
        send[pl.ds(at, part), :] = jnp.where(on_first, later, carry)


def small(kernel, tokens, args, outs):
    return pl.pallas_call(
        functools.partial(kernel, tokens=tokens),
        out_shape=[jax.ShapeDtypeStruct((rows, DH), F32) for rows in outs],
        in_specs=[VMEM] * len(args),
        out_specs=[VMEM] * len(outs),
        compiler_params=params(4),
        cost_estimate=pl.CostEstimate(flops=0, bytes_accessed=2 * MIB, transcendentals=0),
    )(*args)


def local_kernel(starts_ref, q_ref, k_ref, v_ref, out_ref, *, column):
    tokens, width = out_ref.shape
    core, _, _, seq = spot()
    half = q_ref.shape[1] // 2
    sides = halves(core, half)
    key_place = lax.broadcasted_iota(jnp.int32, (GROUP, GROUP), 1)
    query_place = lax.broadcasted_iota(jnp.int32, (GROUP, GROUP), 0)
    blocks = tokens // GROUP
    carries = [None] * (width // DH)
    for block in range(blocks):
        rows = slice(block * GROUP, (block + 1) * GROUP)
        first = seq * tokens + block * GROUP
        starts = starts_ref[:, rows]
        begin = jnp.broadcast_to(starts, (DH, GROUP)).T
        valid = (key_place <= query_place) & (key_place + first >= jnp.concatenate([begin, begin], axis=1))
        last = starts[:, GROUP - 1 :]
        keep = query_place[:, :DH] + first >= jnp.broadcast_to(last, (GROUP, DH))
        keep = jnp.where(keep, 1.0, 0.0).astype(jnp.bfloat16)
        usable = jnp.where(begin < first, 1.0, 0.0).astype(jnp.bfloat16)
        go_on = jnp.where(last < first, 1.0, 0.0)
        for head in range(width // DH):
            col = column + head * DH
            q = q_ref[rows, pl.ds(sides[col // half] + col % half, DH)]
            k, v = k_ref[rows, col : col + DH], v_ref[rows, col : col + DH]
            scores = lax.dot_general(q, k, (((1,), (1,)), ((), ())), preferred_element_type=F32)
            scores = jnp.where(valid, scores, 0.0).astype(jnp.bfloat16)
            if block < blocks - 1:
                both = jnp.dot(
                    jnp.concatenate([scores, (k * keep).T], axis=0), v, preferred_element_type=F32
                )
                attn, state = both[:GROUP], both[GROUP:]
            else:
                attn, state = jnp.dot(scores, v, preferred_element_type=F32), None
            if block:
                attn = attn + jnp.dot(q * usable, carries[head].astype(jnp.bfloat16), preferred_element_type=F32)
            out_ref[rows, head * DH : (head + 1) * DH] = attn
            if state is not None:
                carries[head] = state if block == 0 else state + go_on * carries[head]


def local_attention(starts, queries, keys, values, column, wide):
    tokens = queries.shape[0]
    return pl.pallas_call(
        functools.partial(local_kernel, column=column),
        out_shape=pltpu.VMEM((tokens, wide), F32),
        in_specs=[VMEM] * 4,
        out_specs=VMEM,
        compiler_params=params(4),
        cost_estimate=pl.CostEstimate(
            flops=wide * tokens * (4 * GROUP + 4 * DH), bytes_accessed=tokens * wide * 10, transcendentals=0
        ),
    )(starts, in_vmem(queries), in_vmem(keys), in_vmem(values))


def finish_kernel(starts_ref, q_ref, carry, *refs, places, kept, rows, count):
    locals_ = refs[:count]
    before = refs[count] if len(refs) == count + 4 else None
    out, squares, states = refs[-3:]
    tokens, half = out.shape
    core, _, _, seq = spot()
    side = halves(core, half)[kept]
    opened = jnp.sum((starts_ref[...] < seq * tokens).astype(jnp.int32))
    states[...] = jnp.zeros_like(states)
    for head in range(half // DH):
        span = slice(head % 2 * DH, (head % 2 + 1) * DH)
        states[head // 2, span, span] = carry[head * DH : (head + 1) * DH, :].astype(jnp.bfloat16)

    def step(index, _):
        start = pl.multiple_of(index * rows, rows)
        span = pl.ds(start, rows)
        usable = start + lax.broadcasted_iota(jnp.int32, (rows, 2 * DH), 0) < opened
        total = jnp.zeros((rows, DH), F32)
        for pair in range(half // (2 * DH)):
            q = q_ref[span, pl.ds(side + pair * 2 * DH, 2 * DH)]
            inter = jnp.where(usable, jnp.dot(q, states[pair], preferred_element_type=F32), 0.0)
            for head in range(2):
                part, col = places[2 * pair + head]
                attn = locals_[part][span, col : col + DH] + inter[:, head * DH : (head + 1) * DH]
                at = (2 * pair + head) * DH
                out[span, at : at + DH] = attn
                total = total + attn * attn
        summed = jnp.sum(total.T, axis=0, keepdims=True)
        squares[:, span] = summed if before is None else summed + before[:, span]
        return 0

    lax.fori_loop(0, tokens // rows, step, 0)


def finish(starts, queries, carry, locals_, places, kept, before):
    tokens, width = queries.shape
    half = width // 2
    extra = [] if before is None else [before]
    return pl.pallas_call(
        functools.partial(finish_kernel, places=places, kept=kept, rows=tokens, count=len(locals_)),
        out_shape=[pltpu.VMEM((tokens, half), F32), pltpu.VMEM((1, tokens), F32)],
        in_specs=[VMEM] * (3 + len(locals_) + len(extra)),
        out_specs=[VMEM] * 2,
        scratch_shapes=[pltpu.VMEM((half // (2 * DH), 2 * DH, 2 * DH), jnp.bfloat16)],
        compiler_params=params(8),
        cost_estimate=pl.CostEstimate(
            flops=tokens * width * DH, bytes_accessed=tokens * width * 3, transcendentals=0
        ),
    )(starts, in_vmem(queries), carry, *[in_vmem(part) for part in locals_], *extra)


def norm_kernel(sq0, sq1, sq2, sq3, gain_ref, away, keep, out, buffer, gains, factors, sems, *, rows):
    tokens, width = out.shape
    half = width // 2
    sides = halves(spot()[0], half)

    def copies(index):
        at = pl.ds(pl.multiple_of(index * rows, rows), rows)
        return [
            pltpu.make_async_copy(
                buffer.at[at, number * half : (number + 1) * half], out.at[at, pl.ds(side, half)], sems.at[number, index]
            )
            for number, side in enumerate(sides)
        ]

    for number, side in enumerate(sides):
        gains[:, number * half : (number + 1) * half] = gain_ref[:, pl.ds(side, half)]

    total = (sq0[...] + sq1[...]) + (sq2[...] + sq3[...])
    factors[...] = jnp.broadcast_to(lax.rsqrt(total / (HEADS * DH) + EPS), (DH, tokens)).T

    def step(index, _):
        span = pl.ds(pl.multiple_of(index * rows, rows), rows)
        factor = factors[span, :]
        for number, (ref, copy) in enumerate(zip((away, keep), copies(index))):
            for col in range(0, half, DH):
                cols = slice(number * half + col, number * half + col + DH)
                value = ref[span, col : col + DH] * factor * gains[:, cols]
                buffer[span, cols] = value.astype(jnp.bfloat16)
            copy.start()
        return 0

    steps = tokens // rows
    lax.fori_loop(0, steps, step, 0)
    for index in range(steps):
        for copy in copies(index):
            copy.wait()


def normalise(squares, gain, away, keep):
    tokens, half = away.shape
    width = 2 * half
    rows = DH
    return pl.pallas_call(
        functools.partial(norm_kernel, rows=rows),
        out_shape=jax.ShapeDtypeStruct((tokens, width), jnp.bfloat16),
        in_specs=[VMEM] * 7,
        out_specs=ANY,
        scratch_shapes=[
            pltpu.VMEM((tokens, width), jnp.bfloat16),
            pltpu.VMEM((1, width), F32),
            pltpu.VMEM((tokens, DH), F32),
            pltpu.SemaphoreType.DMA((2, tokens // rows)),
        ],
        compiler_params=params(8),
        cost_estimate=pl.CostEstimate(flops=2 * tokens * width, bytes_accessed=6 * tokens * width, transcendentals=0),
    )(*squares, gain, in_vmem(away), in_vmem(keep))


def on_device(queries, keys, values, doc_start, norm_gain):
    tokens, width = queries.shape
    half = width // 2
    heads = width // DH

    away, keys, values, starts = own_states(doc_start, keys, values)
    recv = swap_cores(away)
    keep = kept_states(starts, keys, values)
    queries = after(queries, away)
    part = half // SEQ_Y

    shares = [3 * heads // 8, 5 * heads // 16, 5 * heads // 16]
    places_ = [(part, col * DH) for part, share in enumerate(shares) for col in range(share)]

    def local(number, gate):
        column = sum(shares[:number]) * DH
        return local_attention(after(starts, gate), queries, keys, values, column, shares[number] * DH)

    mine = small(cores_kernel, tokens, (keep, recv), [part + 8] * SEQ_Y)
    rows = [mine[0]] + [turn_row(mine[d], d) for d in (1, 2, 3)]
    first = local(0, mine[0])
    rows[3], first = lax.optimization_barrier((rows[3], first))
    (whole,) = small(row_kernel, tokens, rows, [part])
    ups = [swap_rows(whole, d) for d in (3, 2, 1)]
    second = local(1, whole)
    ups[2], second = lax.optimization_barrier((ups[2], second))
    carries = small(carry_kernel, tokens, (*rows, *ups), [part] * SEQ_Y)
    got = [carries[0]] + [turn_row(carries[d], d) for d in (1, 2, 3)]
    third = local(2, carries[0])
    got[3], third = lax.optimization_barrier((got[3], third))
    own, send = small(spread_kernel, tokens, (*got, keep, recv), [part * SEQ_Y] * 2)
    other = swap_cores(send)
    locals_ = [first, second, third]
    kept_attn, kept_squares = finish(starts, queries, own, locals_, places_[heads // 2 :], 1, None)
    other, kept_squares = lax.optimization_barrier((other, kept_squares))
    away_attn, squares = finish(starts, queries, other, locals_, places_[: heads // 2], 0, kept_squares)
    sums = [squares] + [
        lax.ppermute(squares, "head", [(z, z ^ d) for z in range(4)]) for d in (3, 2, 1)
    ]
    return normalise(sums, norm_gain.reshape(1, width), away_attn, kept_attn)


def solution(mesh):
    return jax.shard_map(
        on_device,
        mesh=mesh,
        in_specs=(P("seq", "head"), P("seq", "head"), P("seq", "head"), P("seq"), P("head")),
        out_specs=P("seq", "head"),
        check_vma=False,
    )
```

```python
import functools

import jax
import jax.numpy as jnp
from jax import lax
from jax.experimental import pallas as pl
from jax.experimental.pallas import tpu as pltpu
from jax.sharding import PartitionSpec as P

HEADS = 64
DH = 128
GROUP = 256
EPS = 1e-06
SEQ_Y = 4
SEQ_X = 4
MIB = 1 << 20
ANY = pl.BlockSpec(memory_space=pl.ANY)
VMEM = pl.BlockSpec(memory_space=pltpu.VMEM)
SMEM = pl.BlockSpec(memory_space=pltpu.SMEM)
F32 = jnp.float32


def device_of(x, y, core):
    return (x * SEQ_Y + y) * 2 + core


def places():
    return [(x, y, c) for x in range(SEQ_X) for y in range(SEQ_Y) for c in range(2)]


def swap_cores(value):
    return lax.ppermute(
        value, "seq", [(device_of(x, y, c), device_of(x, y, 1 - c)) for x, y, c in places()]
    )


def turn_row(value, steps):
    return lax.ppermute(
        value,
        "seq",
        [(device_of(x, y, c), device_of(x, (y + steps) % SEQ_Y, c)) for x, y, c in places()],
    )


def swap_rows(value, steps):
    return lax.ppermute(
        value, "seq", [(device_of(x, y, c), device_of(x ^ steps, y, c)) for x, y, c in places()]
    )


def params(limit):
    return pltpu.CompilerParams(vmem_limit_bytes=limit * MIB)


def in_hbm(value):
    return pltpu.with_memory_space_constraint(value, pltpu.HBM)


def in_vmem(value):
    return pltpu.with_memory_space_constraint(value, pltpu.VMEM)


def after(value, *others):
    return lax.optimization_barrier((value, *others))[0]


def spot():
    seq = lax.axis_index("seq")
    chip = lax.div(seq, 2)
    return lax.rem(seq, 2), lax.rem(chip, SEQ_Y), lax.div(chip, SEQ_Y), seq


def halves(core, half):
    return [pl.multiple_of(side * half, half) for side in (1 - core, core)]


def state_kernel(starts_hbm, k_hbm, v_hbm, away, k_ref, v_ref, starts, sems, starts_sem, *, rows):
    tokens, width = k_ref.shape
    half = width // 2
    core, _, _, seq = spot()
    base = seq * tokens
    starts_copy = pltpu.make_async_copy(starts_hbm, starts.at[0], starts_sem)
    spans = [slice(start, start + rows) for start in range(0, tokens, rows)]
    copies = [
        [
            pltpu.make_async_copy(
                source.at[span, pl.ds(side, half)],
                ref.at[span, index * half : (index + 1) * half],
                sems.at[2 * number + index, step],
            )
            for number, (source, ref) in enumerate(((k_hbm, k_ref), (v_hbm, v_ref)))
        ]
        for index, side in enumerate(halves(core, half))
        for step, span in enumerate(spans)
    ]
    starts_copy.start()
    for group in copies:
        for copy in group:
            copy.start()
    row = lax.broadcasted_iota(jnp.int32, (8, DH), 0)
    place = base + lax.broadcasted_iota(jnp.int32, (rows, 2 * DH), 0)
    starts_copy.wait()
    first = jnp.broadcast_to(starts[:, :1], (1, DH))
    last = jnp.broadcast_to(starts[:, tokens - 1 :], (1, DH))
    away[half:, :] = jnp.where(row == 0, first, last).astype(F32)
    last = jnp.broadcast_to(starts[:, tokens - 1 :], (rows, 2 * DH))
    for step, span in enumerate(spans):
        for copy in copies[step]:
            copy.wait()
        kept = jnp.where(place + step * rows >= last, 1.0, 0.0).astype(jnp.bfloat16)
        add_states(away, k_ref, v_ref, span, kept, 0, step == 0)
    for group in copies[len(spans) :]:
        for copy in group:
            copy.wait()


def add_states(out, k_ref, v_ref, span, kept, column, first):
    for col in range(0, out.shape[0] - 8, 2 * DH):
        cols = slice(column + col, column + col + 2 * DH)
        both = lax.dot_general(
            k_ref[span, cols] * kept, v_ref[span, cols], (((0,), (0,)), ((), ())), preferred_element_type=F32
        )
        for head in range(2):
            lanes = slice(head * DH, (head + 1) * DH)
            at = slice(col + head * DH, col + (head + 1) * DH)
            if first:
                out[at, :] = both[lanes, lanes]
            else:
                out[at, :] += both[lanes, lanes]


def keep_kernel(starts, k_ref, v_ref, keep, *, rows):
    tokens, width = k_ref.shape
    half = width // 2
    base = spot()[3] * tokens
    row = lax.broadcasted_iota(jnp.int32, (8, DH), 0)
    first = jnp.broadcast_to(starts[:, :1], (1, DH))
    last = jnp.broadcast_to(starts[:, tokens - 1 :], (1, DH))
    keep[half:, :] = jnp.where(row == 0, first, last).astype(F32)
    place = base + lax.broadcasted_iota(jnp.int32, (rows, 2 * DH), 0)
    last = jnp.broadcast_to(starts[:, tokens - 1 :], (rows, 2 * DH))
    for start in range(0, tokens, rows):
        kept = jnp.where(place + start >= last, 1.0, 0.0).astype(jnp.bfloat16)
        add_states(keep, k_ref, v_ref, slice(start, start + rows), kept, half, start == 0)


def own_states(starts, keys, values):
    tokens, width = keys.shape
    rows = 6 * GROUP
    held = pltpu.VMEM((tokens, width), jnp.bfloat16)
    return pl.pallas_call(
        functools.partial(state_kernel, rows=rows),
        out_shape=[pltpu.VMEM((width // 2 + 8, DH), F32), held, held, pltpu.VMEM((1, tokens), jnp.int32)],
        in_specs=[ANY, ANY, ANY],
        out_specs=[VMEM] * 4,
        scratch_shapes=[pltpu.SemaphoreType.DMA((4, tokens // rows)), pltpu.SemaphoreType.DMA],
        compiler_params=params(4),
        cost_estimate=pl.CostEstimate(
            flops=tokens * width * DH, bytes_accessed=4 * tokens * width, transcendentals=0
        ),
    )(in_hbm(starts), in_hbm(keys), in_hbm(values))


def kept_states(starts, keys, values):
    tokens, width = keys.shape
    return pl.pallas_call(
        functools.partial(keep_kernel, rows=2 * GROUP),
        out_shape=pltpu.VMEM((width // 2 + 8, DH), F32),
        in_specs=[VMEM] * 3,
        out_specs=VMEM,
        compiler_params=params(4),
        cost_estimate=pl.CostEstimate(flops=tokens * width * DH, bytes_accessed=2 * tokens * width, transcendentals=0),
    )(starts, in_vmem(keys), in_vmem(values))


def marks(ref):
    at = ref.shape[0] - 8
    return ref[at : at + 1, :], ref[at + 1 : at + 2, :]


def chip_edges(tokens, seq):
    first = lax.div(seq, 2) * (2 * tokens)
    return first.astype(F32), (first + tokens).astype(F32)


def cores_kernel(keep, recv, own, to1, to2, to3, *, tokens):
    total = keep.shape[0] - 8
    part = total // SEQ_Y
    core, y, _, seq = spot()
    on_first = core == 0
    k_first, k_last = marks(keep)
    r_first, r_last = marks(recv)
    first = jnp.where(on_first, k_first, r_first)
    last = jnp.where(on_first, r_last, k_last)
    edge = chip_edges(tokens, seq)[1]
    joined = jnp.where(last < edge, 1.0, 0.0)
    w_keep = jnp.where(on_first, joined, 1.0)
    w_recv = jnp.where(on_first, 1.0, joined)
    row = lax.broadcasted_iota(jnp.int32, (8, DH), 0)
    flags = jnp.where(row == 0, first, last)
    for steps, out in enumerate((own, to1, to2, to3)):
        at = pl.multiple_of(lax.rem(y + steps, SEQ_Y) * part, part)
        out[:part, :] = keep[pl.ds(at, part), :] * w_keep + recv[pl.ds(at, part), :] * w_recv
        out[part:, :] = flags


def sources(y):
    return [lax.rem(y + SEQ_Y - d, SEQ_Y) for d in range(SEQ_Y)]


def ends(tokens, x, place):
    return ((x * SEQ_Y + place + 1) * (2 * tokens)).astype(F32)


def row_kernel(own, from1, from2, from3, out, *, tokens):
    part = out.shape[0]
    refs = (own, from1, from2, from3)
    _, y, x, _ = spot()
    where = sources(y)
    row_last = jnp.zeros((1, DH), F32)
    for place, ref in zip(where, refs):
        row_last = row_last + jnp.where(place == SEQ_Y - 1, marks(ref)[1], 0.0)
    total = jnp.zeros((part, DH), F32)
    for place, ref in zip(where, refs):
        total = total + ref[:part, :] * jnp.where(row_last < ends(tokens, x, place), 1.0, 0.0)
    out[...] = total


def carry_kernel(own, from1, from2, from3, up3, up2, up1, out0, out1, out2, out3, *, tokens):
    part = out0.shape[0]
    refs = (own, from1, from2, from3)
    ups = (up3, up2, up1)
    _, y, x, _ = spot()
    where = sources(y)
    for steps, out in enumerate((out0, out1, out2, out3)):
        target = (SEQ_Y - steps) % SEQ_Y
        place = where[target]
        first = marks(refs[target])[0]
        total = jnp.zeros((part, DH), F32)
        for source in range(SEQ_Y):
            if source != target:
                before = jnp.where(where[source] < place, 1.0, 0.0)
                weight = jnp.where(first < ends(tokens, x, where[source]), before, 0.0)
                total = total + refs[source][:part, :] * weight
        for steps, ref in zip((1, 2, 3), ups):
            row = x ^ steps
            before = jnp.where(row < x, 1.0, 0.0)
            total = total + ref[...] * jnp.where(first < ends(tokens, row, SEQ_Y - 1), before, 0.0)
        out[...] = total


def spread_kernel(own, got1, got2, got3, keep, recv, mine, send, *, tokens):
    part = own.shape[0]
    core, y, _, seq = spot()
    on_first = core == 0
    chip, edge = chip_edges(tokens, seq)
    second_first = jnp.where(on_first, marks(recv)[0], marks(keep)[0])
    w_state = jnp.where(second_first < edge, 1.0, 0.0)
    w_carry = jnp.where(second_first < chip, 1.0, 0.0)
    w_keep = jnp.where(on_first, w_state, 0.0)
    w_recv = jnp.where(on_first, 0.0, w_state)
    for place, ref in zip(sources(y), (own, got1, got2, got3)):
        at = pl.multiple_of(place * part, part)
        carry = ref[...]
        later = keep[pl.ds(at, part), :] * w_keep + recv[pl.ds(at, part), :] * w_recv + carry * w_carry
        mine[pl.ds(at, part), :] = jnp.where(on_first, carry, later)
        send[pl.ds(at, part), :] = jnp.where(on_first, later, carry)


def small(kernel, tokens, args, outs):
    return pl.pallas_call(
        functools.partial(kernel, tokens=tokens),
        out_shape=[jax.ShapeDtypeStruct((rows, DH), F32) for rows in outs],
        in_specs=[VMEM] * len(args),
        out_specs=[VMEM] * len(outs),
        compiler_params=params(4),
        cost_estimate=pl.CostEstimate(flops=0, bytes_accessed=2 * MIB, transcendentals=0),
    )(*args)


def local_kernel(starts_ref, q_ref, k_ref, v_ref, out_ref, *, column):
    tokens, width = out_ref.shape
    core, _, _, seq = spot()
    half = q_ref.shape[1] // 2
    sides = halves(core, half)
    key_place = lax.broadcasted_iota(jnp.int32, (GROUP, GROUP), 1)
    query_place = lax.broadcasted_iota(jnp.int32, (GROUP, GROUP), 0)
    blocks = tokens // GROUP
    carries = [None] * (width // DH)
    for block in range(blocks):
        rows = slice(block * GROUP, (block + 1) * GROUP)
        first = seq * tokens + block * GROUP
        starts = starts_ref[:, rows]
        begin = jnp.broadcast_to(starts, (DH, GROUP)).T
        valid = (key_place <= query_place) & (key_place + first >= jnp.concatenate([begin, begin], axis=1))
        last = starts[:, GROUP - 1 :]
        keep = query_place[:, :DH] + first >= jnp.broadcast_to(last, (GROUP, DH))
        keep = jnp.where(keep, 1.0, 0.0).astype(jnp.bfloat16)
        usable = jnp.where(begin < first, 1.0, 0.0).astype(jnp.bfloat16)
        go_on = jnp.where(last < first, 1.0, 0.0)
        for head in range(width // DH):
            col = column + head * DH
            q = q_ref[rows, pl.ds(sides[col // half] + col % half, DH)]
            k, v = k_ref[rows, col : col + DH], v_ref[rows, col : col + DH]
            scores = lax.dot_general(q, k, (((1,), (1,)), ((), ())), preferred_element_type=F32)
            scores = jnp.where(valid, scores, 0.0).astype(jnp.bfloat16)
            if block < blocks - 1:
                both = jnp.dot(
                    jnp.concatenate([scores, (k * keep).T], axis=0), v, preferred_element_type=F32
                )
                attn, state = both[:GROUP], both[GROUP:]
            else:
                attn, state = jnp.dot(scores, v, preferred_element_type=F32), None
            if block:
                attn = attn + jnp.dot(q * usable, carries[head].astype(jnp.bfloat16), preferred_element_type=F32)
            out_ref[rows, head * DH : (head + 1) * DH] = attn
            if state is not None:
                carries[head] = state if block == 0 else state + go_on * carries[head]


def local_attention(starts, queries, keys, values, column, wide):
    tokens = queries.shape[0]
    return pl.pallas_call(
        functools.partial(local_kernel, column=column),
        out_shape=pltpu.VMEM((tokens, wide), F32),
        in_specs=[VMEM] * 4,
        out_specs=VMEM,
        compiler_params=params(4),
        cost_estimate=pl.CostEstimate(
            flops=wide * tokens * (4 * GROUP + 4 * DH), bytes_accessed=tokens * wide * 10, transcendentals=0
        ),
    )(starts, in_vmem(queries), in_vmem(keys), in_vmem(values))


def finish_kernel(starts_ref, q_ref, carry, *refs, places, kept, rows, count):
    locals_ = refs[:count]
    before = refs[count] if len(refs) == count + 4 else None
    out, squares, states = refs[-3:]
    tokens, half = out.shape
    core, _, _, seq = spot()
    side = halves(core, half)[kept]
    opened = jnp.sum((starts_ref[...] < seq * tokens).astype(jnp.int32))
    states[...] = jnp.zeros_like(states)
    for head in range(half // DH):
        span = slice(head % 2 * DH, (head % 2 + 1) * DH)
        states[head // 2, span, span] = carry[head * DH : (head + 1) * DH, :].astype(jnp.bfloat16)

    def step(index, _):
        start = pl.multiple_of(index * rows, rows)
        span = pl.ds(start, rows)
        usable = start + lax.broadcasted_iota(jnp.int32, (rows, 2 * DH), 0) < opened
        total = jnp.zeros((rows, DH), F32)
        for pair in range(half // (2 * DH)):
            q = q_ref[span, pl.ds(side + pair * 2 * DH, 2 * DH)]
            inter = jnp.where(usable, jnp.dot(q, states[pair], preferred_element_type=F32), 0.0)
            for head in range(2):
                part, col = places[2 * pair + head]
                attn = locals_[part][span, col : col + DH] + inter[:, head * DH : (head + 1) * DH]
                at = (2 * pair + head) * DH
                out[span, at : at + DH] = attn
                total = total + attn * attn
        summed = jnp.sum(total.T, axis=0, keepdims=True)
        squares[:, span] = summed if before is None else summed + before[:, span]
        return 0

    lax.fori_loop(0, tokens // rows, step, 0)


def finish(starts, queries, carry, locals_, places, kept, before):
    tokens, width = queries.shape
    half = width // 2
    extra = [] if before is None else [before]
    return pl.pallas_call(
        functools.partial(finish_kernel, places=places, kept=kept, rows=tokens, count=len(locals_)),
        out_shape=[pltpu.VMEM((tokens, half), F32), pltpu.VMEM((1, tokens), F32)],
        in_specs=[VMEM] * (3 + len(locals_) + len(extra)),
        out_specs=[VMEM] * 2,
        scratch_shapes=[pltpu.VMEM((half // (2 * DH), 2 * DH, 2 * DH), jnp.bfloat16)],
        compiler_params=params(8),
        cost_estimate=pl.CostEstimate(
            flops=tokens * width * DH, bytes_accessed=tokens * width * 3, transcendentals=0
        ),
    )(starts, in_vmem(queries), carry, *[in_vmem(part) for part in locals_], *extra)


def norm_kernel(sq0, sq1, sq2, sq3, gain_ref, away, keep, out, buffer, gains, factors, sems, *, rows):
    tokens, width = out.shape
    half = width // 2
    sides = halves(spot()[0], half)

    def copies(index):
        at = pl.ds(pl.multiple_of(index * rows, rows), rows)
        return [
            pltpu.make_async_copy(
                buffer.at[at, number * half : (number + 1) * half], out.at[at, pl.ds(side, half)], sems.at[number, index]
            )
            for number, side in enumerate(sides)
        ]

    for number, side in enumerate(sides):
        gains[:, number * half : (number + 1) * half] = gain_ref[:, pl.ds(side, half)]

    total = (sq0[...] + sq1[...]) + (sq2[...] + sq3[...])
    factors[...] = jnp.broadcast_to(lax.rsqrt(total / (HEADS * DH) + EPS), (DH, tokens)).T

    def step(index, _):
        span = pl.ds(pl.multiple_of(index * rows, rows), rows)
        factor = factors[span, :]
        for number, (ref, copy) in enumerate(zip((away, keep), copies(index))):
            for col in range(0, half, DH):
                cols = slice(number * half + col, number * half + col + DH)
                value = ref[span, col : col + DH] * factor * gains[:, cols]
                buffer[span, cols] = value.astype(jnp.bfloat16)
            copy.start()
        return 0

    steps = tokens // rows
    lax.fori_loop(0, steps, step, 0)
    for index in range(steps):
        for copy in copies(index):
            copy.wait()


def normalise(squares, gain, away, keep):
    tokens, half = away.shape
    width = 2 * half
    rows = DH
    return pl.pallas_call(
        functools.partial(norm_kernel, rows=rows),
        out_shape=jax.ShapeDtypeStruct((tokens, width), jnp.bfloat16),
        in_specs=[VMEM] * 7,
        out_specs=ANY,
        scratch_shapes=[
            pltpu.VMEM((tokens, width), jnp.bfloat16),
            pltpu.VMEM((1, width), F32),
            pltpu.VMEM((tokens, DH), F32),
            pltpu.SemaphoreType.DMA((2, tokens // rows)),
        ],
        compiler_params=params(8),
        cost_estimate=pl.CostEstimate(flops=2 * tokens * width, bytes_accessed=6 * tokens * width, transcendentals=0),
    )(*squares, gain, in_vmem(away), in_vmem(keep))


def on_device(queries, keys, values, doc_start, norm_gain):
    tokens, width = queries.shape
    half = width // 2
    heads = width // DH

    away, keys, values, starts = own_states(doc_start, keys, values)
    recv = swap_cores(away)
    keep = kept_states(starts, keys, values)
    queries = after(queries, away)
    part = half // SEQ_Y

    shares = [3 * heads // 8, 5 * heads // 16, 5 * heads // 16]
    places_ = [(part, col * DH) for part, share in enumerate(shares) for col in range(share)]

    def local(number, gate):
        column = sum(shares[:number]) * DH
        return local_attention(after(starts, gate), queries, keys, values, column, shares[number] * DH)

    mine = small(cores_kernel, tokens, (keep, recv), [part + 8] * SEQ_Y)
    rows = [mine[0]] + [turn_row(mine[d], d) for d in (1, 2, 3)]
    first = local(0, mine[0])
    rows[3], first = lax.optimization_barrier((rows[3], first))
    (whole,) = small(row_kernel, tokens, rows, [part])
    ups = [swap_rows(whole, d) for d in (1, 2, 3)]
    second = local(1, whole)
    ups[2], second = lax.optimization_barrier((ups[2], second))
    carries = small(carry_kernel, tokens, (*rows, *ups), [part] * SEQ_Y)
    got = [carries[0]] + [turn_row(carries[d], d) for d in (1, 2, 3)]
    third = local(2, carries[0])
    got[3], third = lax.optimization_barrier((got[3], third))
    own, send = small(spread_kernel, tokens, (*got, keep, recv), [part * SEQ_Y] * 2)
    other = swap_cores(send)
    locals_ = [first, second, third]
    kept_attn, kept_squares = finish(starts, queries, own, locals_, places_[heads // 2 :], 1, None)
    other, kept_squares = lax.optimization_barrier((other, kept_squares))
    away_attn, squares = finish(starts, queries, other, locals_, places_[: heads // 2], 0, kept_squares)
    sums = [squares] + [
        lax.ppermute(squares, "head", [(z, (z + d) % 4) for z in range(4)]) for d in (1, 2, 3)
    ]
    return normalise(sums, norm_gain.reshape(1, width), away_attn, kept_attn)


def solution(mesh):
    return jax.shard_map(
        on_device,
        mesh=mesh,
        in_specs=(P("seq", "head"), P("seq", "head"), P("seq", "head"), P("seq"), P("head")),
        out_specs=P("seq", "head"),
        check_vma=False,
    )
```

```python
import functools

import jax
import jax.numpy as jnp
from jax import lax
from jax.experimental import pallas as pl
from jax.experimental.pallas import tpu as pltpu
from jax.sharding import PartitionSpec as P

HEADS = 64
DH = 128
GROUP = 256
EPS = 1e-06
SEQ_Y = 4
SEQ_X = 4
MIB = 1 << 20
ANY = pl.BlockSpec(memory_space=pl.ANY)
VMEM = pl.BlockSpec(memory_space=pltpu.VMEM)
SMEM = pl.BlockSpec(memory_space=pltpu.SMEM)
F32 = jnp.float32


def device_of(x, y, core):
    return (x * SEQ_Y + y) * 2 + core


def places():
    return [(x, y, c) for x in range(SEQ_X) for y in range(SEQ_Y) for c in range(2)]


def swap_cores(value):
    return lax.ppermute(
        value, "seq", [(device_of(x, y, c), device_of(x, y, 1 - c)) for x, y, c in places()]
    )


def turn_row(value, steps):
    return lax.ppermute(
        value,
        "seq",
        [(device_of(x, y, c), device_of(x, (y + steps) % SEQ_Y, c)) for x, y, c in places()],
    )


def swap_rows(value, steps):
    return lax.ppermute(
        value, "seq", [(device_of(x, y, c), device_of(x ^ steps, y, c)) for x, y, c in places()]
    )


def params(limit):
    return pltpu.CompilerParams(vmem_limit_bytes=limit * MIB)


def in_hbm(value):
    return pltpu.with_memory_space_constraint(value, pltpu.HBM)


def in_vmem(value):
    return pltpu.with_memory_space_constraint(value, pltpu.VMEM)


def after(value, *others):
    return lax.optimization_barrier((value, *others))[0]


def spot():
    seq = lax.axis_index("seq")
    chip = lax.div(seq, 2)
    return lax.rem(seq, 2), lax.rem(chip, SEQ_Y), lax.div(chip, SEQ_Y), seq


def halves(core, half):
    return [pl.multiple_of(side * half, half) for side in (1 - core, core)]


def state_kernel(starts_hbm, k_hbm, v_hbm, away, k_ref, v_ref, starts, sems, starts_sem, *, rows):
    tokens, width = k_ref.shape
    half = width // 2
    core, _, _, seq = spot()
    base = seq * tokens
    starts_copy = pltpu.make_async_copy(starts_hbm, starts.at[0], starts_sem)
    spans = [slice(start, start + rows) for start in range(0, tokens, rows)]
    copies = [
        [
            pltpu.make_async_copy(
                source.at[span, pl.ds(side, half)],
                ref.at[span, index * half : (index + 1) * half],
                sems.at[2 * number + index, step],
            )
            for number, (source, ref) in enumerate(((k_hbm, k_ref), (v_hbm, v_ref)))
        ]
        for index, side in enumerate(halves(core, half))
        for step, span in enumerate(spans)
    ]
    starts_copy.start()
    for group in copies:
        for copy in group:
            copy.start()
    row = lax.broadcasted_iota(jnp.int32, (8, DH), 0)
    place = base + lax.broadcasted_iota(jnp.int32, (rows, 2 * DH), 0)
    starts_copy.wait()
    first = jnp.broadcast_to(starts[:, :1], (1, DH))
    last = jnp.broadcast_to(starts[:, tokens - 1 :], (1, DH))
    away[half:, :] = jnp.where(row == 0, first, last).astype(F32)
    last = jnp.broadcast_to(starts[:, tokens - 1 :], (rows, 2 * DH))
    for step, span in enumerate(spans):
        for copy in copies[step]:
            copy.wait()
        kept = jnp.where(place + step * rows >= last, 1.0, 0.0).astype(jnp.bfloat16)
        add_states(away, k_ref, v_ref, span, kept, 0, step == 0)
    for group in copies[len(spans) :]:
        for copy in group:
            copy.wait()


def add_states(out, k_ref, v_ref, span, kept, column, first):
    for col in range(0, out.shape[0] - 8, 2 * DH):
        cols = slice(column + col, column + col + 2 * DH)
        both = lax.dot_general(
            k_ref[span, cols] * kept, v_ref[span, cols], (((0,), (0,)), ((), ())), preferred_element_type=F32
        )
        for head in range(2):
            lanes = slice(head * DH, (head + 1) * DH)
            at = slice(col + head * DH, col + (head + 1) * DH)
            if first:
                out[at, :] = both[lanes, lanes]
            else:
                out[at, :] += both[lanes, lanes]


def keep_kernel(starts, k_ref, v_ref, keep, *, rows):
    tokens, width = k_ref.shape
    half = width // 2
    base = spot()[3] * tokens
    row = lax.broadcasted_iota(jnp.int32, (8, DH), 0)
    first = jnp.broadcast_to(starts[:, :1], (1, DH))
    last = jnp.broadcast_to(starts[:, tokens - 1 :], (1, DH))
    keep[half:, :] = jnp.where(row == 0, first, last).astype(F32)
    place = base + lax.broadcasted_iota(jnp.int32, (rows, 2 * DH), 0)
    last = jnp.broadcast_to(starts[:, tokens - 1 :], (rows, 2 * DH))
    for start in range(0, tokens, rows):
        kept = jnp.where(place + start >= last, 1.0, 0.0).astype(jnp.bfloat16)
        add_states(keep, k_ref, v_ref, slice(start, start + rows), kept, half, start == 0)


def own_states(starts, keys, values):
    tokens, width = keys.shape
    rows = 6 * GROUP
    held = pltpu.VMEM((tokens, width), jnp.bfloat16)
    return pl.pallas_call(
        functools.partial(state_kernel, rows=rows),
        out_shape=[pltpu.VMEM((width // 2 + 8, DH), F32), held, held, pltpu.VMEM((1, tokens), jnp.int32)],
        in_specs=[ANY, ANY, ANY],
        out_specs=[VMEM] * 4,
        scratch_shapes=[pltpu.SemaphoreType.DMA((4, tokens // rows)), pltpu.SemaphoreType.DMA],
        compiler_params=params(4),
        cost_estimate=pl.CostEstimate(
            flops=tokens * width * DH, bytes_accessed=4 * tokens * width, transcendentals=0
        ),
    )(in_hbm(starts), in_hbm(keys), in_hbm(values))


def kept_states(starts, keys, values):
    tokens, width = keys.shape
    return pl.pallas_call(
        functools.partial(keep_kernel, rows=2 * GROUP),
        out_shape=pltpu.VMEM((width // 2 + 8, DH), F32),
        in_specs=[VMEM] * 3,
        out_specs=VMEM,
        compiler_params=params(4),
        cost_estimate=pl.CostEstimate(flops=tokens * width * DH, bytes_accessed=2 * tokens * width, transcendentals=0),
    )(starts, in_vmem(keys), in_vmem(values))


def marks(ref):
    at = ref.shape[0] - 8
    return ref[at : at + 1, :], ref[at + 1 : at + 2, :]


def chip_edges(tokens, seq):
    first = lax.div(seq, 2) * (2 * tokens)
    return first.astype(F32), (first + tokens).astype(F32)


def cores_kernel(keep, recv, own, to1, to2, to3, *, tokens):
    total = keep.shape[0] - 8
    part = total // SEQ_Y
    core, y, _, seq = spot()
    on_first = core == 0
    k_first, k_last = marks(keep)
    r_first, r_last = marks(recv)
    first = jnp.where(on_first, k_first, r_first)
    last = jnp.where(on_first, r_last, k_last)
    edge = chip_edges(tokens, seq)[1]
    joined = jnp.where(last < edge, 1.0, 0.0)
    w_keep = jnp.where(on_first, joined, 1.0)
    w_recv = jnp.where(on_first, 1.0, joined)
    row = lax.broadcasted_iota(jnp.int32, (8, DH), 0)
    flags = jnp.where(row == 0, first, last)
    for steps, out in enumerate((own, to1, to2, to3)):
        at = pl.multiple_of(lax.rem(y + steps, SEQ_Y) * part, part)
        out[:part, :] = keep[pl.ds(at, part), :] * w_keep + recv[pl.ds(at, part), :] * w_recv
        out[part:, :] = flags


def sources(y):
    return [lax.rem(y + SEQ_Y - d, SEQ_Y) for d in range(SEQ_Y)]


def ends(tokens, x, place):
    return ((x * SEQ_Y + place + 1) * (2 * tokens)).astype(F32)


def row_kernel(own, from1, from2, from3, out, *, tokens):
    part = out.shape[0]
    refs = (own, from1, from2, from3)
    _, y, x, _ = spot()
    where = sources(y)
    row_last = jnp.zeros((1, DH), F32)
    for place, ref in zip(where, refs):
        row_last = row_last + jnp.where(place == SEQ_Y - 1, marks(ref)[1], 0.0)
    total = jnp.zeros((part, DH), F32)
    for place, ref in zip(where, refs):
        total = total + ref[:part, :] * jnp.where(row_last < ends(tokens, x, place), 1.0, 0.0)
    out[...] = total


def carry_kernel(own, from1, from2, from3, up3, up2, up1, out0, out1, out2, out3, *, tokens):
    part = out0.shape[0]
    refs = (own, from1, from2, from3)
    ups = (up3, up2, up1)
    _, y, x, _ = spot()
    where = sources(y)
    for steps, out in enumerate((out0, out1, out2, out3)):
        target = (SEQ_Y - steps) % SEQ_Y
        place = where[target]
        first = marks(refs[target])[0]
        total = jnp.zeros((part, DH), F32)
        for source in range(SEQ_Y):
            if source != target:
                before = jnp.where(where[source] < place, 1.0, 0.0)
                weight = jnp.where(first < ends(tokens, x, where[source]), before, 0.0)
                total = total + refs[source][:part, :] * weight
        for steps, ref in zip((1, 3, 2), ups):
            row = x ^ steps
            before = jnp.where(row < x, 1.0, 0.0)
            total = total + ref[...] * jnp.where(first < ends(tokens, row, SEQ_Y - 1), before, 0.0)
        out[...] = total


def spread_kernel(own, got1, got2, got3, keep, recv, mine, send, *, tokens):
    part = own.shape[0]
    core, y, _, seq = spot()
    on_first = core == 0
    chip, edge = chip_edges(tokens, seq)
    second_first = jnp.where(on_first, marks(recv)[0], marks(keep)[0])
    w_state = jnp.where(second_first < edge, 1.0, 0.0)
    w_carry = jnp.where(second_first < chip, 1.0, 0.0)
    w_keep = jnp.where(on_first, w_state, 0.0)
    w_recv = jnp.where(on_first, 0.0, w_state)
    for place, ref in zip(sources(y), (own, got1, got2, got3)):
        at = pl.multiple_of(place * part, part)
        carry = ref[...]
        later = keep[pl.ds(at, part), :] * w_keep + recv[pl.ds(at, part), :] * w_recv + carry * w_carry
        mine[pl.ds(at, part), :] = jnp.where(on_first, carry, later)
        send[pl.ds(at, part), :] = jnp.where(on_first, later, carry)


def small(kernel, tokens, args, outs):
    return pl.pallas_call(
        functools.partial(kernel, tokens=tokens),
        out_shape=[jax.ShapeDtypeStruct((rows, DH), F32) for rows in outs],
        in_specs=[VMEM] * len(args),
        out_specs=[VMEM] * len(outs),
        compiler_params=params(4),
        cost_estimate=pl.CostEstimate(flops=0, bytes_accessed=2 * MIB, transcendentals=0),
    )(*args)


def local_kernel(starts_ref, q_ref, k_ref, v_ref, out_ref, *, column):
    tokens, width = out_ref.shape
    core, _, _, seq = spot()
    half = q_ref.shape[1] // 2
    sides = halves(core, half)
    key_place = lax.broadcasted_iota(jnp.int32, (GROUP, GROUP), 1)
    query_place = lax.broadcasted_iota(jnp.int32, (GROUP, GROUP), 0)
    blocks = tokens // GROUP
    carries = [None] * (width // DH)
    for block in range(blocks):
        rows = slice(block * GROUP, (block + 1) * GROUP)
        first = seq * tokens + block * GROUP
        starts = starts_ref[:, rows]
        begin = jnp.broadcast_to(starts, (DH, GROUP)).T
        valid = (key_place <= query_place) & (key_place + first >= jnp.concatenate([begin, begin], axis=1))
        last = starts[:, GROUP - 1 :]
        keep = query_place[:, :DH] + first >= jnp.broadcast_to(last, (GROUP, DH))
        keep = jnp.where(keep, 1.0, 0.0).astype(jnp.bfloat16)
        usable = jnp.where(begin < first, 1.0, 0.0).astype(jnp.bfloat16)
        go_on = jnp.where(last < first, 1.0, 0.0)
        for head in range(width // DH):
            col = column + head * DH
            q = q_ref[rows, pl.ds(sides[col // half] + col % half, DH)]
            k, v = k_ref[rows, col : col + DH], v_ref[rows, col : col + DH]
            scores = lax.dot_general(q, k, (((1,), (1,)), ((), ())), preferred_element_type=F32)
            scores = jnp.where(valid, scores, 0.0).astype(jnp.bfloat16)
            if block < blocks - 1:
                both = jnp.dot(
                    jnp.concatenate([scores, (k * keep).T], axis=0), v, preferred_element_type=F32
                )
                attn, state = both[:GROUP], both[GROUP:]
            else:
                attn, state = jnp.dot(scores, v, preferred_element_type=F32), None
            if block:
                attn = attn + jnp.dot(q * usable, carries[head].astype(jnp.bfloat16), preferred_element_type=F32)
            out_ref[rows, head * DH : (head + 1) * DH] = attn
            if state is not None:
                carries[head] = state if block == 0 else state + go_on * carries[head]


def local_attention(starts, queries, keys, values, column, wide):
    tokens = queries.shape[0]
    return pl.pallas_call(
        functools.partial(local_kernel, column=column),
        out_shape=pltpu.VMEM((tokens, wide), F32),
        in_specs=[VMEM] * 4,
        out_specs=VMEM,
        compiler_params=params(4),
        cost_estimate=pl.CostEstimate(
            flops=wide * tokens * (4 * GROUP + 4 * DH), bytes_accessed=tokens * wide * 10, transcendentals=0
        ),
    )(starts, in_vmem(queries), in_vmem(keys), in_vmem(values))


def finish_kernel(starts_ref, q_ref, carry, *refs, places, kept, rows, count):
    locals_ = refs[:count]
    before = refs[count] if len(refs) == count + 4 else None
    out, squares, states = refs[-3:]
    tokens, half = out.shape
    core, _, _, seq = spot()
    side = halves(core, half)[kept]
    opened = jnp.sum((starts_ref[...] < seq * tokens).astype(jnp.int32))
    states[...] = jnp.zeros_like(states)
    for head in range(half // DH):
        span = slice(head % 2 * DH, (head % 2 + 1) * DH)
        states[head // 2, span, span] = carry[head * DH : (head + 1) * DH, :].astype(jnp.bfloat16)

    def step(index, _):
        start = pl.multiple_of(index * rows, rows)
        span = pl.ds(start, rows)
        usable = start + lax.broadcasted_iota(jnp.int32, (rows, 2 * DH), 0) < opened
        total = jnp.zeros((rows, DH), F32)
        for pair in range(half // (2 * DH)):
            q = q_ref[span, pl.ds(side + pair * 2 * DH, 2 * DH)]
            inter = jnp.where(usable, jnp.dot(q, states[pair], preferred_element_type=F32), 0.0)
            for head in range(2):
                part, col = places[2 * pair + head]
                attn = locals_[part][span, col : col + DH] + inter[:, head * DH : (head + 1) * DH]
                at = (2 * pair + head) * DH
                out[span, at : at + DH] = attn
                total = total + attn * attn
        summed = jnp.sum(total.T, axis=0, keepdims=True)
        squares[:, span] = summed if before is None else summed + before[:, span]
        return 0

    lax.fori_loop(0, tokens // rows, step, 0)


def finish(starts, queries, carry, locals_, places, kept, before):
    tokens, width = queries.shape
    half = width // 2
    extra = [] if before is None else [before]
    return pl.pallas_call(
        functools.partial(finish_kernel, places=places, kept=kept, rows=tokens, count=len(locals_)),
        out_shape=[pltpu.VMEM((tokens, half), F32), pltpu.VMEM((1, tokens), F32)],
        in_specs=[VMEM] * (3 + len(locals_) + len(extra)),
        out_specs=[VMEM] * 2,
        scratch_shapes=[pltpu.VMEM((half // (2 * DH), 2 * DH, 2 * DH), jnp.bfloat16)],
        compiler_params=params(8),
        cost_estimate=pl.CostEstimate(
            flops=tokens * width * DH, bytes_accessed=tokens * width * 3, transcendentals=0
        ),
    )(starts, in_vmem(queries), carry, *[in_vmem(part) for part in locals_], *extra)


def norm_kernel(sq0, sq1, sq2, sq3, gain_ref, away, keep, out, buffer, gains, factors, sems, *, rows):
    tokens, width = out.shape
    half = width // 2
    sides = halves(spot()[0], half)

    def copies(index):
        at = pl.ds(pl.multiple_of(index * rows, rows), rows)
        return [
            pltpu.make_async_copy(
                buffer.at[at, number * half : (number + 1) * half], out.at[at, pl.ds(side, half)], sems.at[number, index]
            )
            for number, side in enumerate(sides)
        ]

    for number, side in enumerate(sides):
        gains[:, number * half : (number + 1) * half] = gain_ref[:, pl.ds(side, half)]

    total = (sq0[...] + sq1[...]) + (sq2[...] + sq3[...])
    factors[...] = jnp.broadcast_to(lax.rsqrt(total / (HEADS * DH) + EPS), (DH, tokens)).T

    def step(index, _):
        span = pl.ds(pl.multiple_of(index * rows, rows), rows)
        factor = factors[span, :]
        for number, (ref, copy) in enumerate(zip((away, keep), copies(index))):
            for col in range(0, half, DH):
                cols = slice(number * half + col, number * half + col + DH)
                value = ref[span, col : col + DH] * factor * gains[:, cols]
                buffer[span, cols] = value.astype(jnp.bfloat16)
            copy.start()
        return 0

    steps = tokens // rows
    lax.fori_loop(0, steps, step, 0)
    for index in range(steps):
        for copy in copies(index):
            copy.wait()


def normalise(squares, gain, away, keep):
    tokens, half = away.shape
    width = 2 * half
    rows = DH
    return pl.pallas_call(
        functools.partial(norm_kernel, rows=rows),
        out_shape=jax.ShapeDtypeStruct((tokens, width), jnp.bfloat16),
        in_specs=[VMEM] * 7,
        out_specs=ANY,
        scratch_shapes=[
            pltpu.VMEM((tokens, width), jnp.bfloat16),
            pltpu.VMEM((1, width), F32),
            pltpu.VMEM((tokens, DH), F32),
            pltpu.SemaphoreType.DMA((2, tokens // rows)),
        ],
        compiler_params=params(8),
        cost_estimate=pl.CostEstimate(flops=2 * tokens * width, bytes_accessed=6 * tokens * width, transcendentals=0),
    )(*squares, gain, in_vmem(away), in_vmem(keep))


def on_device(queries, keys, values, doc_start, norm_gain):
    tokens, width = queries.shape
    half = width // 2
    heads = width // DH

    away, keys, values, starts = own_states(doc_start, keys, values)
    recv = swap_cores(away)
    keep = kept_states(starts, keys, values)
    queries = after(queries, away)
    part = half // SEQ_Y

    shares = [3 * heads // 8, 5 * heads // 16, 5 * heads // 16]
    places_ = [(part, col * DH) for part, share in enumerate(shares) for col in range(share)]

    def local(number, gate):
        column = sum(shares[:number]) * DH
        return local_attention(after(starts, gate), queries, keys, values, column, shares[number] * DH)

    mine = small(cores_kernel, tokens, (keep, recv), [part + 8] * SEQ_Y)
    rows = [mine[0]] + [turn_row(mine[d], d) for d in (1, 2, 3)]
    first = local(0, mine[0])
    rows[3], first = lax.optimization_barrier((rows[3], first))
    (whole,) = small(row_kernel, tokens, rows, [part])
    ups = [swap_rows(whole, d) for d in (1, 3, 2)]
    second = local(1, whole)
    ups[2], second = lax.optimization_barrier((ups[2], second))
    carries = small(carry_kernel, tokens, (*rows, *ups), [part] * SEQ_Y)
    got = [carries[0]] + [turn_row(carries[d], d) for d in (1, 2, 3)]
    third = local(2, carries[0])
    got[3], third = lax.optimization_barrier((got[3], third))
    own, send = small(spread_kernel, tokens, (*got, keep, recv), [part * SEQ_Y] * 2)
    other = swap_cores(send)
    locals_ = [first, second, third]
    kept_attn, kept_squares = finish(starts, queries, own, locals_, places_[heads // 2 :], 1, None)
    other, kept_squares = lax.optimization_barrier((other, kept_squares))
    away_attn, squares = finish(starts, queries, other, locals_, places_[: heads // 2], 0, kept_squares)
    sums = [squares] + [
        lax.ppermute(squares, "head", [(z, (z + d) % 4) for z in range(4)]) for d in (3, 2, 1)
    ]
    return normalise(sums, norm_gain.reshape(1, width), away_attn, kept_attn)


def solution(mesh):
    return jax.shard_map(
        on_device,
        mesh=mesh,
        in_specs=(P("seq", "head"), P("seq", "head"), P("seq", "head"), P("seq"), P("head")),
        out_specs=P("seq", "head"),
        check_vma=False,
    )
```

```python
import functools

import jax
import jax.numpy as jnp
from jax import lax
from jax.experimental import pallas as pl
from jax.experimental.pallas import tpu as pltpu
from jax.sharding import PartitionSpec as P

HEADS = 64
DH = 128
GROUP = 256
EPS = 1e-06
SEQ_Y = 4
SEQ_X = 4
MIB = 1 << 20
ANY = pl.BlockSpec(memory_space=pl.ANY)
VMEM = pl.BlockSpec(memory_space=pltpu.VMEM)
SMEM = pl.BlockSpec(memory_space=pltpu.SMEM)
F32 = jnp.float32


def device_of(x, y, core):
    return (x * SEQ_Y + y) * 2 + core


def places():
    return [(x, y, c) for x in range(SEQ_X) for y in range(SEQ_Y) for c in range(2)]


def swap_cores(value):
    return lax.ppermute(
        value, "seq", [(device_of(x, y, c), device_of(x, y, 1 - c)) for x, y, c in places()]
    )


def turn_row(value, steps):
    return lax.ppermute(
        value,
        "seq",
        [(device_of(x, y, c), device_of(x, (y + steps) % SEQ_Y, c)) for x, y, c in places()],
    )


def swap_rows(value, steps):
    return lax.ppermute(
        value, "seq", [(device_of(x, y, c), device_of(x ^ steps, y, c)) for x, y, c in places()]
    )


def params(limit):
    return pltpu.CompilerParams(vmem_limit_bytes=limit * MIB)


def in_hbm(value):
    return pltpu.with_memory_space_constraint(value, pltpu.HBM)


def in_vmem(value):
    return pltpu.with_memory_space_constraint(value, pltpu.VMEM)


def after(value, *others):
    return lax.optimization_barrier((value, *others))[0]


def spot():
    seq = lax.axis_index("seq")
    chip = lax.div(seq, 2)
    return lax.rem(seq, 2), lax.rem(chip, SEQ_Y), lax.div(chip, SEQ_Y), seq


def halves(core, half):
    return [pl.multiple_of(side * half, half) for side in (1 - core, core)]


def state_kernel(starts_hbm, k_hbm, v_hbm, away, k_ref, v_ref, starts, sems, starts_sem, *, rows):
    tokens, width = k_ref.shape
    half = width // 2
    core, _, _, seq = spot()
    base = seq * tokens
    starts_copy = pltpu.make_async_copy(starts_hbm, starts.at[0], starts_sem)
    spans = [slice(start, start + rows) for start in range(0, tokens, rows)]
    copies = [
        [
            pltpu.make_async_copy(
                source.at[span, pl.ds(side, half)],
                ref.at[span, index * half : (index + 1) * half],
                sems.at[2 * number + index, step],
            )
            for number, (source, ref) in enumerate(((k_hbm, k_ref), (v_hbm, v_ref)))
        ]
        for index, side in enumerate(halves(core, half))
        for step, span in enumerate(spans)
    ]
    starts_copy.start()
    for group in copies:
        for copy in group:
            copy.start()
    row = lax.broadcasted_iota(jnp.int32, (8, DH), 0)
    place = base + lax.broadcasted_iota(jnp.int32, (rows, 2 * DH), 0)
    starts_copy.wait()
    first = jnp.broadcast_to(starts[:, :1], (1, DH))
    last = jnp.broadcast_to(starts[:, tokens - 1 :], (1, DH))
    away[half:, :] = jnp.where(row == 0, first, last).astype(F32)
    last = jnp.broadcast_to(starts[:, tokens - 1 :], (rows, 2 * DH))
    for step, span in enumerate(spans):
        for copy in copies[step]:
            copy.wait()
        kept = jnp.where(place + step * rows >= last, 1.0, 0.0).astype(jnp.bfloat16)
        add_states(away, k_ref, v_ref, span, kept, 0, step == 0)
    for group in copies[len(spans) :]:
        for copy in group:
            copy.wait()


def add_states(out, k_ref, v_ref, span, kept, column, first):
    for col in range(0, out.shape[0] - 8, 2 * DH):
        cols = slice(column + col, column + col + 2 * DH)
        both = lax.dot_general(
            k_ref[span, cols] * kept, v_ref[span, cols], (((0,), (0,)), ((), ())), preferred_element_type=F32
        )
        for head in range(2):
            lanes = slice(head * DH, (head + 1) * DH)
            at = slice(col + head * DH, col + (head + 1) * DH)
            if first:
                out[at, :] = both[lanes, lanes]
            else:
                out[at, :] += both[lanes, lanes]


def keep_kernel(starts, k_ref, v_ref, keep, *, rows):
    tokens, width = k_ref.shape
    half = width // 2
    base = spot()[3] * tokens
    row = lax.broadcasted_iota(jnp.int32, (8, DH), 0)
    first = jnp.broadcast_to(starts[:, :1], (1, DH))
    last = jnp.broadcast_to(starts[:, tokens - 1 :], (1, DH))
    keep[half:, :] = jnp.where(row == 0, first, last).astype(F32)
    place = base + lax.broadcasted_iota(jnp.int32, (rows, 2 * DH), 0)
    last = jnp.broadcast_to(starts[:, tokens - 1 :], (rows, 2 * DH))
    for start in range(0, tokens, rows):
        kept = jnp.where(place + start >= last, 1.0, 0.0).astype(jnp.bfloat16)
        add_states(keep, k_ref, v_ref, slice(start, start + rows), kept, half, start == 0)


def own_states(starts, keys, values):
    tokens, width = keys.shape
    rows = 6 * GROUP
    held = pltpu.VMEM((tokens, width), jnp.bfloat16)
    return pl.pallas_call(
        functools.partial(state_kernel, rows=rows),
        out_shape=[pltpu.VMEM((width // 2 + 8, DH), F32), held, held, pltpu.VMEM((1, tokens), jnp.int32)],
        in_specs=[ANY, ANY, ANY],
        out_specs=[VMEM] * 4,
        scratch_shapes=[pltpu.SemaphoreType.DMA((4, tokens // rows)), pltpu.SemaphoreType.DMA],
        compiler_params=params(4),
        cost_estimate=pl.CostEstimate(
            flops=tokens * width * DH, bytes_accessed=4 * tokens * width, transcendentals=0
        ),
    )(in_hbm(starts), in_hbm(keys), in_hbm(values))


def kept_states(starts, keys, values):
    tokens, width = keys.shape
    return pl.pallas_call(
        functools.partial(keep_kernel, rows=2 * GROUP),
        out_shape=pltpu.VMEM((width // 2 + 8, DH), F32),
        in_specs=[VMEM] * 3,
        out_specs=VMEM,
        compiler_params=params(4),
        cost_estimate=pl.CostEstimate(flops=tokens * width * DH, bytes_accessed=2 * tokens * width, transcendentals=0),
    )(starts, in_vmem(keys), in_vmem(values))


def marks(ref):
    at = ref.shape[0] - 8
    return ref[at : at + 1, :], ref[at + 1 : at + 2, :]


def chip_edges(tokens, seq):
    first = lax.div(seq, 2) * (2 * tokens)
    return first.astype(F32), (first + tokens).astype(F32)


def cores_kernel(keep, recv, own, to1, to2, to3, *, tokens):
    total = keep.shape[0] - 8
    part = total // SEQ_Y
    core, y, _, seq = spot()
    on_first = core == 0
    k_first, k_last = marks(keep)
    r_first, r_last = marks(recv)
    first = jnp.where(on_first, k_first, r_first)
    last = jnp.where(on_first, r_last, k_last)
    edge = chip_edges(tokens, seq)[1]
    joined = jnp.where(last < edge, 1.0, 0.0)
    w_keep = jnp.where(on_first, joined, 1.0)
    w_recv = jnp.where(on_first, 1.0, joined)
    row = lax.broadcasted_iota(jnp.int32, (8, DH), 0)
    flags = jnp.where(row == 0, first, last)
    for steps, out in enumerate((own, to1, to2, to3)):
        at = pl.multiple_of(lax.rem(y + steps, SEQ_Y) * part, part)
        out[:part, :] = keep[pl.ds(at, part), :] * w_keep + recv[pl.ds(at, part), :] * w_recv
        out[part:, :] = flags


def sources(y):
    return [lax.rem(y + SEQ_Y - d, SEQ_Y) for d in range(SEQ_Y)]


def ends(tokens, x, place):
    return ((x * SEQ_Y + place + 1) * (2 * tokens)).astype(F32)


def row_kernel(own, from1, from2, from3, out, *, tokens):
    part = out.shape[0]
    refs = (own, from1, from2, from3)
    _, y, x, _ = spot()
    where = sources(y)
    row_last = jnp.zeros((1, DH), F32)
    for place, ref in zip(where, refs):
        row_last = row_last + jnp.where(place == SEQ_Y - 1, marks(ref)[1], 0.0)
    total = jnp.zeros((part, DH), F32)
    for place, ref in zip(where, refs):
        total = total + ref[:part, :] * jnp.where(row_last < ends(tokens, x, place), 1.0, 0.0)
    out[...] = total


def carry_kernel(own, from1, from2, from3, up3, up2, up1, out0, out1, out2, out3, *, tokens):
    part = out0.shape[0]
    refs = (own, from1, from2, from3)
    ups = (up3, up2, up1)
    _, y, x, _ = spot()
    where = sources(y)
    for steps, out in enumerate((out0, out1, out2, out3)):
        target = (SEQ_Y - steps) % SEQ_Y
        place = where[target]
        first = marks(refs[target])[0]
        total = jnp.zeros((part, DH), F32)
        for source in range(SEQ_Y):
            if source != target:
                before = jnp.where(where[source] < place, 1.0, 0.0)
                weight = jnp.where(first < ends(tokens, x, where[source]), before, 0.0)
                total = total + refs[source][:part, :] * weight
        for steps, ref in zip((1, 3, 2), ups):
            row = x ^ steps
            before = jnp.where(row < x, 1.0, 0.0)
            total = total + ref[...] * jnp.where(first < ends(tokens, row, SEQ_Y - 1), before, 0.0)
        out[...] = total


def spread_kernel(own, got1, got2, got3, keep, recv, mine, send, *, tokens):
    part = own.shape[0]
    core, y, _, seq = spot()
    on_first = core == 0
    chip, edge = chip_edges(tokens, seq)
    second_first = jnp.where(on_first, marks(recv)[0], marks(keep)[0])
    w_state = jnp.where(second_first < edge, 1.0, 0.0)
    w_carry = jnp.where(second_first < chip, 1.0, 0.0)
    w_keep = jnp.where(on_first, w_state, 0.0)
    w_recv = jnp.where(on_first, 0.0, w_state)
    for place, ref in zip(sources(y), (own, got1, got2, got3)):
        at = pl.multiple_of(place * part, part)
        carry = ref[...]
        later = keep[pl.ds(at, part), :] * w_keep + recv[pl.ds(at, part), :] * w_recv + carry * w_carry
        mine[pl.ds(at, part), :] = jnp.where(on_first, carry, later)
        send[pl.ds(at, part), :] = jnp.where(on_first, later, carry)


def small(kernel, tokens, args, outs):
    return pl.pallas_call(
        functools.partial(kernel, tokens=tokens),
        out_shape=[jax.ShapeDtypeStruct((rows, DH), F32) for rows in outs],
        in_specs=[VMEM] * len(args),
        out_specs=[VMEM] * len(outs),
        compiler_params=params(4),
        cost_estimate=pl.CostEstimate(flops=0, bytes_accessed=2 * MIB, transcendentals=0),
    )(*args)


def local_kernel(starts_ref, q_ref, k_ref, v_ref, out_ref, *, column):
    tokens, width = out_ref.shape
    core, _, _, seq = spot()
    half = q_ref.shape[1] // 2
    sides = halves(core, half)
    key_place = lax.broadcasted_iota(jnp.int32, (GROUP, GROUP), 1)
    query_place = lax.broadcasted_iota(jnp.int32, (GROUP, GROUP), 0)
    blocks = tokens // GROUP
    carries = [None] * (width // DH)
    for block in range(blocks):
        rows = slice(block * GROUP, (block + 1) * GROUP)
        first = seq * tokens + block * GROUP
        starts = starts_ref[:, rows]
        begin = jnp.broadcast_to(starts, (DH, GROUP)).T
        valid = (key_place <= query_place) & (key_place + first >= jnp.concatenate([begin, begin], axis=1))
        last = starts[:, GROUP - 1 :]
        keep = query_place[:, :DH] + first >= jnp.broadcast_to(last, (GROUP, DH))
        keep = jnp.where(keep, 1.0, 0.0).astype(jnp.bfloat16)
        usable = jnp.where(begin < first, 1.0, 0.0).astype(jnp.bfloat16)
        go_on = jnp.where(last < first, 1.0, 0.0)
        for head in range(width // DH):
            col = column + head * DH
            q = q_ref[rows, pl.ds(sides[col // half] + col % half, DH)]
            k, v = k_ref[rows, col : col + DH], v_ref[rows, col : col + DH]
            scores = lax.dot_general(q, k, (((1,), (1,)), ((), ())), preferred_element_type=F32)
            scores = jnp.where(valid, scores, 0.0).astype(jnp.bfloat16)
            if block < blocks - 1:
                both = jnp.dot(
                    jnp.concatenate([scores, (k * keep).T], axis=0), v, preferred_element_type=F32
                )
                attn, state = both[:GROUP], both[GROUP:]
            else:
                attn, state = jnp.dot(scores, v, preferred_element_type=F32), None
            if block:
                attn = attn + jnp.dot(q * usable, carries[head].astype(jnp.bfloat16), preferred_element_type=F32)
            out_ref[rows, head * DH : (head + 1) * DH] = attn
            if state is not None:
                carries[head] = state if block == 0 else state + go_on * carries[head]


def local_attention(starts, queries, keys, values, column, wide):
    tokens = queries.shape[0]
    return pl.pallas_call(
        functools.partial(local_kernel, column=column),
        out_shape=pltpu.VMEM((tokens, wide), F32),
        in_specs=[VMEM] * 4,
        out_specs=VMEM,
        compiler_params=params(4),
        cost_estimate=pl.CostEstimate(
            flops=wide * tokens * (4 * GROUP + 4 * DH), bytes_accessed=tokens * wide * 10, transcendentals=0
        ),
    )(starts, in_vmem(queries), in_vmem(keys), in_vmem(values))


def finish_kernel(starts_ref, q_ref, carry, *refs, places, kept, rows, count):
    locals_ = refs[:count]
    before = refs[count] if len(refs) == count + 4 else None
    out, squares, states = refs[-3:]
    tokens, half = out.shape
    core, _, _, seq = spot()
    side = halves(core, half)[kept]
    opened = jnp.sum((starts_ref[...] < seq * tokens).astype(jnp.int32))
    states[...] = jnp.zeros_like(states)
    for head in range(half // DH):
        span = slice(head % 2 * DH, (head % 2 + 1) * DH)
        states[head // 2, span, span] = carry[head * DH : (head + 1) * DH, :].astype(jnp.bfloat16)

    def step(index, _):
        start = pl.multiple_of(index * rows, rows)
        span = pl.ds(start, rows)
        usable = start + lax.broadcasted_iota(jnp.int32, (rows, 2 * DH), 0) < opened
        total = jnp.zeros((rows, DH), F32)
        for pair in range(half // (2 * DH)):
            q = q_ref[span, pl.ds(side + pair * 2 * DH, 2 * DH)]
            inter = jnp.where(usable, jnp.dot(q, states[pair], preferred_element_type=F32), 0.0)
            for head in range(2):
                part, col = places[2 * pair + head]
                attn = locals_[part][span, col : col + DH] + inter[:, head * DH : (head + 1) * DH]
                at = (2 * pair + head) * DH
                out[span, at : at + DH] = attn
                total = total + attn * attn
        summed = jnp.sum(total.T, axis=0, keepdims=True)
        squares[:, span] = summed if before is None else summed + before[:, span]
        return 0

    lax.fori_loop(0, tokens // rows, step, 0)


def finish(starts, queries, carry, locals_, places, kept, before):
    tokens, width = queries.shape
    half = width // 2
    extra = [] if before is None else [before]
    return pl.pallas_call(
        functools.partial(finish_kernel, places=places, kept=kept, rows=tokens, count=len(locals_)),
        out_shape=[pltpu.VMEM((tokens, half), F32), pltpu.VMEM((1, tokens), F32)],
        in_specs=[VMEM] * (3 + len(locals_) + len(extra)),
        out_specs=[VMEM] * 2,
        scratch_shapes=[pltpu.VMEM((half // (2 * DH), 2 * DH, 2 * DH), jnp.bfloat16)],
        compiler_params=params(8),
        cost_estimate=pl.CostEstimate(
            flops=tokens * width * DH, bytes_accessed=tokens * width * 3, transcendentals=0
        ),
    )(starts, in_vmem(queries), carry, *[in_vmem(part) for part in locals_], *extra)


def norm_kernel(sq0, sq1, sq2, sq3, gain_ref, away, keep, out, buffer, gains, factors, sems, *, rows):
    tokens, width = out.shape
    half = width // 2
    sides = halves(spot()[0], half)

    def copies(index):
        at = pl.ds(pl.multiple_of(index * rows, rows), rows)
        return [
            pltpu.make_async_copy(
                buffer.at[at, number * half : (number + 1) * half], out.at[at, pl.ds(side, half)], sems.at[number, index]
            )
            for number, side in enumerate(sides)
        ]

    for number, side in enumerate(sides):
        gains[:, number * half : (number + 1) * half] = gain_ref[:, pl.ds(side, half)]

    total = (sq0[...] + sq1[...]) + (sq2[...] + sq3[...])
    factors[...] = jnp.broadcast_to(lax.rsqrt(total / (HEADS * DH) + EPS), (DH, tokens)).T

    def step(index, _):
        span = pl.ds(pl.multiple_of(index * rows, rows), rows)
        factor = factors[span, :]
        for number, (ref, copy) in enumerate(zip((away, keep), copies(index))):
            for col in range(0, half, DH):
                cols = slice(number * half + col, number * half + col + DH)
                value = ref[span, col : col + DH] * factor * gains[:, cols]
                buffer[span, cols] = value.astype(jnp.bfloat16)
            copy.start()
        return 0

    steps = tokens // rows
    lax.fori_loop(0, steps, step, 0, unroll=2)
    for index in range(steps):
        for copy in copies(index):
            copy.wait()


def normalise(squares, gain, away, keep):
    tokens, half = away.shape
    width = 2 * half
    rows = DH
    return pl.pallas_call(
        functools.partial(norm_kernel, rows=rows),
        out_shape=jax.ShapeDtypeStruct((tokens, width), jnp.bfloat16),
        in_specs=[VMEM] * 7,
        out_specs=ANY,
        scratch_shapes=[
            pltpu.VMEM((tokens, width), jnp.bfloat16),
            pltpu.VMEM((1, width), F32),
            pltpu.VMEM((tokens, DH), F32),
            pltpu.SemaphoreType.DMA((2, tokens // rows)),
        ],
        compiler_params=params(8),
        cost_estimate=pl.CostEstimate(flops=2 * tokens * width, bytes_accessed=6 * tokens * width, transcendentals=0),
    )(*squares, gain, in_vmem(away), in_vmem(keep))


def on_device(queries, keys, values, doc_start, norm_gain):
    tokens, width = queries.shape
    half = width // 2
    heads = width // DH

    away, keys, values, starts = own_states(doc_start, keys, values)
    recv = swap_cores(away)
    keep = kept_states(starts, keys, values)
    queries = after(queries, away)
    part = half // SEQ_Y

    shares = [3 * heads // 8, 5 * heads // 16, 5 * heads // 16]
    places_ = [(part, col * DH) for part, share in enumerate(shares) for col in range(share)]

    def local(number, gate):
        column = sum(shares[:number]) * DH
        return local_attention(after(starts, gate), queries, keys, values, column, shares[number] * DH)

    mine = small(cores_kernel, tokens, (keep, recv), [part + 8] * SEQ_Y)
    rows = [mine[0]] + [turn_row(mine[d], d) for d in (1, 2, 3)]
    first = local(0, mine[0])
    rows[3], first = lax.optimization_barrier((rows[3], first))
    (whole,) = small(row_kernel, tokens, rows, [part])
    ups = [swap_rows(whole, d) for d in (1, 3, 2)]
    second = local(1, whole)
    ups[2], second = lax.optimization_barrier((ups[2], second))
    carries = small(carry_kernel, tokens, (*rows, *ups), [part] * SEQ_Y)
    got = [carries[0]] + [turn_row(carries[d], d) for d in (1, 2, 3)]
    third = local(2, carries[0])
    got[3], third = lax.optimization_barrier((got[3], third))
    own, send = small(spread_kernel, tokens, (*got, keep, recv), [part * SEQ_Y] * 2)
    other = swap_cores(send)
    locals_ = [first, second, third]
    kept_attn, kept_squares = finish(starts, queries, own, locals_, places_[heads // 2 :], 1, None)
    other, kept_squares = lax.optimization_barrier((other, kept_squares))
    away_attn, squares = finish(starts, queries, other, locals_, places_[: heads // 2], 0, kept_squares)
    sums = [squares] + [
        lax.ppermute(squares, "head", [(z, (z + d) % 4) for z in range(4)]) for d in (3, 2, 1)
    ]
    return normalise(sums, norm_gain.reshape(1, width), away_attn, kept_attn)


def solution(mesh):
    return jax.shard_map(
        on_device,
        mesh=mesh,
        in_specs=(P("seq", "head"), P("seq", "head"), P("seq", "head"), P("seq"), P("head")),
        out_specs=P("seq", "head"),
        check_vma=False,
    )
```
